512 devices in a mesh: leaf: 512 (over z, x, y, core).
Axes of the slice: x: 4, y: 8, z: 8, core: 2. Of those that a mesh axis runs over, the one named last changes fastest.
Arguments:
- embeddings: bfloat16 [1048576, 256], P('leaf'), may hold values from -12 to 12
- rhs: bfloat16 [1048576, 64], P('leaf'), may hold values from -6 to 6
- item_order: int32 [1048576], P('leaf'), may hold values from 0 to 2047, as said below
- leaf_basis: bfloat16 [1048576, 32], P('leaf'), may hold values from -0.375 to 0.375
- leaf_skel: int32 [4096, 32], P('leaf'), may hold values from 0 to 255, as said below
- local_transfer: bfloat16 [7680, 32, 32], P('leaf'), may hold values from -0.875 to 0.875
- local_pick: int32 [3584, 32], P('leaf'), may hold values from 0 to 63, as said below
- upper_transfer: bfloat16 [512, 32, 32], replicated, may hold values from -0.875 to 0.875
- upper_pick: int32 [512, 32], replicated, may hold values from 0 to 63, as said below
Outputs:
- product: bfloat16 [1048576, 64], P('leaf')
The draws below stay inside these ranges and needn't reach their ends.
Inputs may be any that keep to these rules, and one draw needn't show every extreme that they name: `item_order`: each block of 2048 entries is a permutation of 0 to 2047. `leaf_skel`: each row holds 32 different numbers. `local_pick`: each row holds 32 different numbers. `upper_pick`: each row holds 32 different numbers.
All inputs are finite; a program needn't handle non-finite values.
Results may differ from the reference program's by a relative error of at most 0.0043.
Values may be sent and summed in bfloat16 or wider, within the bound.
No kernel may reach another device: no remote copies, remote signals or barrier semaphores. Data moves between devices by JAX's collectives and lax.ppermute only.
A program may use at most 64 MiB of HBM per device.

```python
import math
import jax
import jax.numpy as jnp
from jax import lax

LEAF = 256
EMB = 256
RANK = 32
NRHS = 64
LEAVES_DEV = 8
ITEMS_DEV = 2048
LEAVES = 4096
ITEMS = 1048576
N_LEAF = 512


def distinct_rows(key, rows, count, keep):
    keys = jax.random.split(key, rows)
    perms = jax.vmap(lambda single: jax.random.permutation(single, count))(keys)[:, :keep].astype(jnp.int32)
    inner = jax.random.permutation(jax.random.fold_in(key, 7), count - 2)[:keep - 2].astype(jnp.int32) + 1
    first = jnp.concatenate([jnp.array([0, count - 1], dtype=jnp.int32), inner])
    first = jax.random.permutation(jax.random.fold_in(key, 9), first).astype(jnp.int32)
    return perms.at[0].set(first)


def draw_embeddings(key, part):
    scale_key, base_key = jax.random.split(key)
    scale = jnp.exp(jax.random.uniform(scale_key, (ITEMS, 1), jnp.float32, math.log(0.3), math.log(3.0)))
    base = jnp.clip(jax.random.normal(base_key, (ITEMS, EMB), jnp.float32), -4.0, 4.0)
    return (scale * base).astype(jnp.bfloat16)


def draw_item_order(key, part):
    keys = jax.random.split(key, N_LEAF)
    perms = jax.vmap(lambda single: jax.random.permutation(single, ITEMS_DEV))(keys)
    return perms.reshape(-1).astype(jnp.int32)


def draw_leaf_skel(key, part):
    return distinct_rows(jax.random.fold_in(key, 11), LEAVES, LEAF, RANK)


def draw_local_pick(key, part):
    return distinct_rows(jax.random.fold_in(key, 13), N_LEAF * (LEAVES_DEV - 1), 2 * RANK, RANK)


def draw_upper_pick(key, part):
    return distinct_rows(jax.random.fold_in(key, 17), N_LEAF, 2 * RANK, RANK)


def block_levels(rng, shape, cuts, smallest, largest):
    loudness = 1.0
    for position, shards_of in cuts:
        heights = jax.random.uniform(jax.random.fold_in(jax.random.fold_in(rng, 6), position), (shards_of,), jnp.float32, smallest / len(cuts), largest / len(cuts))
        loudness = loudness * jnp.repeat(jnp.exp(heights), shape[position] // shards_of).reshape((-1,) + (1,) * (len(shape) - 1 - position))
    return loudness


def bell_draw(stream_key, dims, width, most, cuts=(), held_as=jnp.bfloat16):
    loudness = block_levels(stream_key, dims, cuts, -0.22, 0.18) if cuts else 1.0
    entries = jax.random.normal(stream_key, dims, jnp.float32) * width * loudness
    return jnp.minimum(jnp.maximum(entries, -most), most).astype(held_as)


def setup_inputs(seed: int = 0) -> dict:
    seeds = jax.random.split(jax.random.key(seed), 10)
    return {
        "embeddings": draw_embeddings(jax.random.fold_in(seeds[9], 71), 0),
        "rhs": bell_draw(seeds[1], (ITEMS, NRHS), 1.0, 6.0, ((0, 512),)),
        "item_order": draw_item_order(jax.random.fold_in(seeds[9], 71), 0),
        "leaf_basis": bell_draw(seeds[3], (ITEMS, RANK), LEAF ** -0.5, 0.375, ((0, 512),)),
        "leaf_skel": draw_leaf_skel(jax.random.fold_in(seeds[9], 71), 0),
        "local_transfer": bell_draw(seeds[5], (N_LEAF * (2 * LEAVES_DEV - 1), RANK, RANK), (RANK * 17 // 12) ** -0.5, 0.875, ((0, 512),)),
        "local_pick": draw_local_pick(jax.random.fold_in(seeds[9], 71), 0),
        "upper_transfer": bell_draw(seeds[7], (N_LEAF, RANK, RANK), (RANK * 17 // 12) ** -0.5, 0.875),
        "upper_pick": draw_upper_pick(jax.random.fold_in(seeds[9], 71), 0),
    }


RIDGE = 1.0
HIGHEST = lax.Precision.HIGHEST

def kernel_block(left, right):
    left_wide = left.astype(jnp.float32)
    right_wide = right.astype(jnp.float32)
    gram = jnp.einsum('nme,nke->nmk', left_wide, right_wide, precision=HIGHEST)
    left_norm = lax.optimization_barrier(jnp.sum(left_wide * left_wide, axis=-1))
    right_norm = lax.optimization_barrier(jnp.sum(right_wide * right_wide, axis=-1))
    distance = jnp.maximum(left_norm[:, :, None] + right_norm[:, None, :] - 2.0 * gram, 0.0)
    return 1.0 / jnp.sqrt(1.0 + distance / left.shape[-1])

def pair_total(terms):
    paired = terms.reshape((-1, 2) + terms.shape[1:])
    return paired[:, 0] + paired[:, 1]

def pair_select(points, selection):
    joined = points.reshape(-1, 2 * points.shape[1], points.shape[2])
    return jnp.take_along_axis(joined, selection[:, :, None], axis=1)

def swap_pairs(values):
    paired = values.reshape((-1, 2) + values.shape[1:])
    return paired[:, ::-1].reshape(values.shape)

def reference(embeddings, rhs, item_order, leaf_basis, leaf_skel, local_transfer, local_pick, upper_transfer, upper_pick):
    devices = N_LEAF
    per_dev = LEAVES_DEV
    leaves = devices * per_dev
    depth = per_dev.bit_length() - 1
    total = depth + devices.bit_length() - 1
    order = item_order.reshape(devices, -1)
    feats = jnp.take_along_axis(embeddings.reshape(devices, -1, EMB), order[:, :, None], axis=1)
    weights = jnp.take_along_axis(rhs.reshape(devices, -1, NRHS), order[:, :, None], axis=1)
    basis = leaf_basis.reshape(devices, per_dev, LEAF, RANK)

    def leaf_work(inputs):
        feat, weight, base = inputs
        feat = feat.reshape(per_dev, LEAF, EMB)
        weight = weight.reshape(per_dev, LEAF, NRHS).astype(jnp.float32)
        kern = kernel_block(feat, feat) + RIDGE * jnp.eye(LEAF, dtype=jnp.float32)
        rounded = lax.optimization_barrier(kern.astype(jnp.bfloat16)).astype(jnp.float32)
        near_part = jnp.einsum('lij,ljc->lic', rounded, weight, precision=HIGHEST)
        lifted = jnp.einsum('lia,lic->lac', base.astype(jnp.float32), weight, precision=HIGHEST)
        return (near_part, lifted)
    near, leaf_weights = lax.map(leaf_work, (feats, weights, basis))
    near = near.reshape(leaves, LEAF, NRHS)
    leaf_points = jnp.take_along_axis(feats.reshape(leaves, LEAF, EMB), leaf_skel[:, :, None], axis=1)
    local_t = local_transfer.reshape(devices, 2 * per_dev - 1, RANK, RANK)
    local_p = local_pick.reshape(devices, per_dev - 1, RANK)

    def transfer_at(height):
        if height <= depth:
            return local_t[:, (per_dev >> height) - 1:(2 * per_dev >> height) - 1].reshape(-1, RANK, RANK)
        level = height - depth
        return upper_transfer[devices >> level:2 * devices >> level]

    def pick_at(height):
        if height <= depth:
            return local_p[:, (per_dev >> height) - 1:(2 * per_dev >> height) - 1].reshape(-1, RANK)
        level = height - depth
        return upper_pick[devices >> level:2 * devices >> level]
    weight_levels = [leaf_weights.reshape(leaves, RANK, NRHS)]
    point_levels = [leaf_points]
    transfer_levels = [transfer_at(0)]
    for height in range(1, total):
        lifted = jnp.einsum('nab,nac->nbc', transfer_levels[-1].astype(jnp.float32), weight_levels[-1], precision=HIGHEST)
        weight_levels.append(pair_total(lifted))
        point_levels.append(pair_select(point_levels[-1], pick_at(height)))
        transfer_levels.append(transfer_at(height))
    field = None
    for height in reversed(range(total)):
        points = point_levels[height]
        term = jnp.einsum('nmk,nkc->nmc', kernel_block(points, swap_pairs(points)), swap_pairs(weight_levels[height]), precision=HIGHEST)
        if field is not None:
            term = term + jnp.einsum('nab,nbc->nac', transfer_levels[height].astype(jnp.float32), jnp.repeat(field, 2, axis=0), precision=HIGHEST)
        field = term
    far = jnp.einsum('lia,lac->lic', basis.reshape(leaves, LEAF, RANK).astype(jnp.float32), field, precision=HIGHEST)
    result = (near + far).astype(jnp.bfloat16).reshape(devices, ITEMS_DEV, NRHS)
    rows = jnp.arange(devices, dtype=jnp.int32)[:, None]
    product = jnp.zeros_like(result).at[rows, order].set(result)
    return product.reshape(ITEMS, NRHS)
```

```python
import functools

import jax
import jax.numpy as jnp
from jax import lax
from jax.experimental import pallas as pl
from jax.experimental.pallas import tpu as pltpu
from jax.sharding import PartitionSpec as P

RIDGE = 1.0
RADICES = {512: (8, 8, 8)}
F32 = jnp.float32
BF16 = jnp.bfloat16
VMEM_LIMIT = 48 * 1024 * 1024


def dot(a, b):
    return jnp.dot(a, b, preferred_element_type=F32)


def dot_first(a, b):
    return lax.dot_general(a, b, (((0,), (0,)), ((), ())), preferred_element_type=F32)


def dot_last(a, b):
    return lax.dot_general(a, b, (((1,), (1,)), ((), ())), preferred_element_type=F32)


def split(x):
    high = x.astype(BF16)
    return high, (x - high.astype(F32)).astype(BF16)


def dot_wide(a, b):
    a_high, a_low = split(a)
    b_high, b_low = split(b)
    return dot(a_high, b_high) + dot(a_low, b_high) + dot(a_high, b_low)


def dot_right(a, b):
    high, low = split(b)
    return dot(a, high) + dot(a, low)


def dot_first_right(a, b):
    high, low = split(b)
    return dot_first(a, high) + dot_first(a, low)


def iota(shape, axis):
    return lax.broadcasted_iota(jnp.int32, shape, axis)


def one_hot(mask):
    return jnp.where(mask, 1.0, 0.0).astype(BF16)


def kernel_of(distance, width):
    return lax.rsqrt(1.0 + jnp.maximum(distance, 0.0) * (1.0 / width))


def self_kernel(points):
    count, width = points.shape
    gram = dot_last(points, points)
    eye = iota(gram.shape, 0) == iota(gram.shape, 1)
    diagonal = jnp.where(eye, gram, 0.0)
    across = jnp.sum(diagonal, axis=1, keepdims=True)
    down = jnp.sum(diagonal, axis=0, keepdims=True)
    return kernel_of(across + down - 2.0 * gram, width), eye


def columns_of(table):
    return table.astype(F32).T.astype(jnp.int32)


def order_column(order_t, leaf):
    return jnp.concatenate([order_t[:, 2 * leaf : 2 * leaf + 1], order_t[:, 2 * leaf + 1 : 2 * leaf + 2]], axis=0)


def padded_columns(tables, rows):
    stacked = jnp.concatenate(tables, axis=0)
    short = rows - stacked.shape[0]
    if short:
        stacked = jnp.concatenate([stacked, jnp.zeros((short, stacked.shape[1]), jnp.int32)], axis=0)
    wide = jnp.concatenate([stacked, jnp.zeros((rows, 128 - stacked.shape[1]), jnp.int32)], axis=1)
    return columns_of(wide)


def pre_body(leaves, order, rhs, basis, skel, pick, transfer, emb, payload, rhs_tree, points, weights):
    items = rhs.shape[0]
    leaf = items // leaves
    cols = rhs.shape[1]
    rank = skel.shape[1]
    order_t = columns_of(order[...])
    table = padded_columns([skel[...], pick[...]], 16)
    blocks = items // leaf
    joined = jnp.concatenate([rhs[b * leaf : (b + 1) * leaf, :].astype(F32) for b in range(blocks)], axis=1).astype(BF16)
    lane_block = iota((leaf, blocks * cols), 1) // cols
    ids = []
    level = []
    for l in range(leaves):
        column = order_column(order_t, l)
        low, high = column & (leaf - 1), column // leaf
        found = dot(one_hot(low == iota((leaf, leaf), 1)), joined)
        found = jnp.where(high == lane_block, found, 0.0)
        total = found[:, :128]
        for b in range(1, blocks * cols // 128):
            total = total + found[:, b * 128 : (b + 1) * 128]
        picked = total[:, :cols] + total[:, cols:]
        picked = picked.astype(BF16)
        rhs_tree[l * leaf : (l + 1) * leaf, :] = picked
        level.append(dot_first(basis[l * leaf : (l + 1) * leaf, :], picked))
        spot = one_hot(table[:rank, l : l + 1] == iota((rank, leaf), 1))
        digits = jnp.concatenate(
            [jnp.broadcast_to(high, (leaf, 128)), jnp.broadcast_to(low, (leaf, 128))], axis=1
        )
        ids.append(dot(spot, digits.astype(F32).astype(BF16)))
    ids = jnp.concatenate(ids, axis=0).astype(jnp.int32)
    high, low = ids[:, :128], ids[:, 128:]
    lane = iota(high.shape, 1)
    per = leaf // 128
    spots = [one_hot((high == b // per) & (low == lane + 128 * (b % per))) for b in range(items // 128)]
    nodes = dot(jnp.concatenate(spots, axis=1), emb[...]).astype(BF16)
    count = leaves
    at = 0
    while count > 1:
        points[at : at + count * rank, :] = nodes
        weights[at : at + count * rank, :] = jnp.concatenate(level, axis=0)
        at += count * rank
        parents = count // 2
        rows = jnp.concatenate(
            [table[:rank, leaves + q - 1 : leaves + q] + 2 * rank * (q - parents) for q in range(parents, 2 * parents)], axis=0
        )
        nodes = dot(one_hot(rows == iota((parents * rank, count * rank), 1)), nodes).astype(BF16)
        upper = []
        for q in range(parents, 2 * parents):
            pair = jnp.concatenate(level[2 * (q - parents) : 2 * (q - parents) + 2], axis=0)
            moved = transfer[2 * q - 1 : 2 * q + 1].reshape(2 * rank, rank)
            upper.append(dot_first_right(moved, pair))
        level = upper
        count = parents
    own = level[0]
    share = dot_first_right(transfer[0], own)
    tail = jnp.concatenate([own, share], axis=1)
    sent = jnp.concatenate([nodes, tail.astype(BF16)], axis=1)
    for r in range(payload.shape[0]):
        payload[r] = sent


def prep_body(devices, radices, me_ref, pick, own_transfer, *refs):
    rank = own_transfer.shape[1]
    blocks = iter(refs[: sum(n.bit_length() - 1 for n in radices) - 1])
    outs = refs[sum(n.bit_length() - 1 for n in radices) - 1 :]
    selects, lifts, chains = outs[:3]
    select_all, lift_all = outs[3:]
    me = me_ref[0]
    base = 0
    chain = None
    for stage, radix in enumerate(radices):
        depth = radix.bit_length() - 1
        place = (me // (1 << base)) % radix
        wide = radix * rank
        top = (devices + me) // (1 << (base + depth))
        rows = [pick[pl.ds(top * (radix >> h), radix >> h), :] for h in range(1, depth + 1)]
        table = padded_columns(rows, 16)
        moves = [None if stage == 0 and h == 0 else next(blocks) for h in range(depth)]
        eye = iota((wide, wide), 0) == iota((wide, wide), 1)
        select_all[0:wide, :wide] = jnp.where(eye, 1.0, 0.0)
        lift_all[0:wide, :wide] = jnp.where(eye, 1.0, 0.0)
        at, below, column = wide, 0, 0
        starts = [0]
        for h in range(1, depth + 1):
            starts.append(at)
            for p in range(radix >> h):
                pair = slice(below + 2 * rank * p, below + 2 * rank * (p + 1))
                here = slice(at + rank * p, at + rank * (p + 1))
                picked = one_hot(table[:rank, column : column + 1] == iota((rank, 2 * rank), 1))
                select_all[here, :wide] = dot(picked, select_all[pair, :wide].astype(BF16))
                if moves[h - 1] is None:
                    both = iota((2 * rank, rank), 0) % rank == iota((2 * rank, rank), 1)
                    moved = one_hot(both)
                else:
                    moved = moves[h - 1][2 * p : 2 * p + 2].reshape(2 * rank, rank)
                lift_all[here, :wide] = dot_first_right(moved, lift_all[pair, :wide])
                column += 1
            below, at = at, at + rank * (radix >> h)
        spots = [starts[h] + rank * (place // (1 << h)) for h in range(depth)]
        others = [starts[h] + rank * (place // (1 << h) + 1 - 2 * (place // (1 << h) % 2)) for h in range(depth)]
        spots = [pl.multiple_of(s, rank) for s in spots]
        others = [pl.multiple_of(s, rank) for s in others]
        for i, spot in enumerate(spots + others + [starts[depth]]):
            selects[stage, i * rank : (i + 1) * rank, :wide] = select_all[pl.ds(spot, rank), :wide].astype(BF16)
        for i, spot in enumerate(others + [starts[depth]]):
            high, low = split(lift_all[pl.ds(spot, rank), :wide])
            lifts[stage, 0, i * rank : (i + 1) * rank, :wide] = high
            lifts[stage, 1, i * rank : (i + 1) * rank, :wide] = low
        for h in range(depth):
            if chain is None:
                chain = jnp.where(iota((rank, rank), 0) == iota((rank, rank), 1), 1.0, 0.0)
            chains[stage, h * rank : (h + 1) * rank, :] = chain
            if moves[h] is None:
                step = own_transfer[0]
            else:
                step = moves[h][place // (1 << h)]
            high, low = split(chain)
            chain = dot(high, step) + dot(low, step)
        base += depth


def gathered_nodes(stage, depth, rank, cols, gathered, select, lift):
    whole = gathered[...].reshape(gathered.shape[0] * rank, gathered.shape[2])
    width = whole.shape[1] - 2 * cols
    wide = whole.shape[0]
    points = dot(select[:, :wide], whole[:, :width]).astype(BF16)
    tails = whole[:, width:]
    lifted = dot(lift[0, :, :wide], tails) + dot(lift[1, :, :wide], tails)
    if stage == 0:
        first = iota((lifted.shape[0], cols), 0) < rank
        lifted = jnp.where(first, lifted[:, :cols], lifted[:, cols:])
    else:
        lifted = lifted[:, :cols] + lifted[:, cols:]
    return points, lifted


def terms_of(own, other, weights, rank):
    count, width = own.shape
    gram = dot_last(own, other)
    own_wide, other_wide = own.astype(F32), other.astype(F32)
    across = jnp.sum(own_wide * own_wide, axis=1, keepdims=True)
    down = jnp.sum(other_wide * other_wide, axis=1, keepdims=True)
    down = jnp.broadcast_to(down, (count, 128)).T[0:1, :]
    kernel = kernel_of(across + down - 2.0 * gram, width)
    same = iota(gram.shape, 0) // rank == iota(gram.shape, 1) // rank
    return dot_wide(jnp.where(same, kernel, 0.0), weights)


def chained(chain, terms, rank):
    total = None
    for h in range(terms.shape[0] // rank):
        part = dot_wide(chain[h * rank : (h + 1) * rank, :], terms[h * rank : (h + 1) * rank, :])
        total = part if total is None else total + part
    return total


def hop_body(stage, depth, rank, cols, gathered, selects, lifts, payload, pairs, siblings):
    rows = depth * rank
    points, lifted = gathered_nodes(
        stage, depth, rank, cols, gathered, selects[stage, : (2 * depth + 1) * rank, :], lifts[stage, :, : rows + rank, :]
    )
    pairs[...] = points[: 2 * rows, :]
    siblings[...] = lifted[:rows, :]
    high = lifted[rows:, :].astype(BF16).astype(F32)
    tail = jnp.concatenate([high, lifted[rows:, :] - high], axis=1)
    sent = jnp.concatenate([points[2 * rows :, :], tail.astype(BF16)], axis=1)
    for r in range(payload.shape[0]):
        payload[r] = sent


def terms_body(stage, depth, rank, pairs, siblings, chains, before, after):
    rows = depth * rank
    terms = terms_of(pairs[:rows, :], pairs[rows:, :], siblings[...], rank)
    total = chained(chains[stage], terms, rank)
    after[...] = total + before[...] if before is not None else total


def final_body(stage, depth, rank, cols, gathered, selects, lifts, chains, before, spread, product):
    rows = depth * rank
    points, lifted = gathered_nodes(
        stage, depth, rank, cols, gathered, selects[stage, : 2 * rows, :], lifts[stage, :, :rows, :]
    )
    terms = terms_of(points[:rows, :], points[rows:, :], lifted, rank)
    field = chained(chains[stage], terms, rank)
    if before is not None:
        field = field + before[...]
    high = field.astype(BF16).astype(F32)
    low = field - high
    eye = jnp.where(iota((cols, cols), 0) == iota((cols, cols), 1), 1.0, 0.0)
    right = jnp.concatenate([eye, eye, high, high, low, jnp.zeros_like(low)], axis=0).astype(BF16)
    product[...] = dot(spread[...], right).astype(BF16)


def far_body(leaves, rank, cols, points, weights, transfer, result):
    at = 0
    count = leaves
    terms = []
    while count > 1:
        rows = slice(at, at + count * rank)
        kernel, _ = self_kernel(points[rows, :])
        here = iota(kernel.shape, 0) // rank
        there = iota(kernel.shape, 1) // rank
        partner = here + 1 - 2 * (here % 2)
        terms.append(dot_wide(jnp.where(there == partner, kernel, 0.0), weights[rows, :]))
        at += count * rank
        count //= 2
    below = None
    for height in reversed(range(len(terms))):
        count = leaves >> height
        nodes = []
        for n in range(count):
            moved = transfer[count + n - 1]
            term = terms[height][n * rank : (n + 1) * rank, :]
            if below is None:
                node = jnp.concatenate([term, moved.astype(F32), jnp.zeros((rank, 128 - cols - rank), F32)], axis=1)
            else:
                pad = jnp.zeros((rank, 128 - cols), F32)
                node = dot_right(moved, below[n // 2]) + jnp.concatenate([term, pad], axis=1)
            nodes.append(node)
        below = nodes
    result[...] = jnp.concatenate(below, axis=0)


def leaf_body(first, count, rank, order, emb, rhs_tree, basis, far, result):
    items = emb.shape[0]
    leaf = result.shape[0] // count
    cols = rhs_tree.shape[1]
    order_t = columns_of(order[...])
    for i in range(count):
        l = first + i
        rows = slice(l * leaf, (l + 1) * leaf)
        column = order_column(order_t, l)
        feats = dot(one_hot(column == iota((leaf, items), 1)), emb[...]).astype(BF16)
        kernel, eye = self_kernel(feats)
        kernel = jnp.where(eye, kernel + RIDGE, kernel).astype(BF16)
        near = dot(kernel, rhs_tree[rows, :])
        both = dot_right(basis[rows, :], far[l * rank : (l + 1) * rank, :])
        total = near + both[:, :cols]
        total_high = total.astype(BF16).astype(F32)
        moved = both[:, cols : cols + rank]
        moved_high = moved.astype(BF16).astype(F32)
        result[i * leaf : (i + 1) * leaf, :] = jnp.concatenate(
            [total_high, total - total_high, moved_high, moved - moved_high, moved_high, jnp.zeros_like(moved)], axis=1
        ).astype(BF16)


def spread_body(step, order, lower, upper, result):
    chunks = order.shape[0]
    row = jnp.concatenate([order[c : c + 1, :] for c in range(chunks)], axis=1)
    half = lower.shape[0]
    for b in range(result.shape[0] // step):
        mask = row == iota((step, row.shape[1]), 0) + b * step
        hot = one_hot(mask)
        result[b * step : (b + 1) * step, :] = (
            dot(hot[:, :half], lower[...]) + dot(hot[:, half:], upper[...])
        ).astype(BF16)


def call(body, outs, scratch=(), flops=1e8, name=None):
    return pl.pallas_call(
        body,
        out_shape=outs,
        scratch_shapes=list(scratch),
        cost_estimate=pl.CostEstimate(flops=int(flops), bytes_accessed=1 << 20, transcendentals=0),
        compiler_params=pltpu.CompilerParams(vmem_limit_bytes=VMEM_LIMIT),
        name=name,
    )


def shape(dims, dtype):
    return jax.ShapeDtypeStruct(dims, dtype)


def local(
    embeddings,
    rhs,
    item_order,
    leaf_basis,
    leaf_skel,
    local_transfer,
    local_pick,
    upper_transfer,
    upper_pick,
):
    leaves, rank = leaf_skel.shape
    items, cols = rhs.shape
    width = embeddings.shape[1]
    devices = lax.axis_size("leaf")
    radices = RADICES[devices]
    me = lax.axis_index("leaf")
    me = me.astype(jnp.int32).reshape(1)
    order = item_order.reshape(items // 128, 128)
    inner = (2 * leaves - 2) * rank

    payload, rhs_tree, points, weights = call(
        functools.partial(pre_body, leaves),
        (
            shape((radices[0], rank, width + 2 * cols), BF16),
            shape((items, cols), BF16),
            shape((inner, width), BF16),
            shape((inner, cols), F32),
        ),
        name="pre",
    )(order, rhs, leaf_basis, leaf_skel, local_pick, local_transfer, embeddings)

    stages = len(radices)
    most = max(radices)
    depths = [n.bit_length() - 1 for n in radices]
    deepest = max(depths)
    whole = pl.BlockSpec(memory_space=pltpu.VMEM)
    specs = [whole, pl.BlockSpec((1, rank, rank), lambda i, m: (0, 0, 0))]
    base = 0
    for stage, (n, depth) in enumerate(zip(radices, depths)):
        shift = base + depth
        for h in range(depth):
            if stage or h:
                specs.append(
                    pl.BlockSpec((n >> h, rank, rank), functools.partial(lambda s, i, m: ((devices + m[0]) // (1 << s), 0, 0), shift))
                )
        base += depth
    selects, lifts, chains = pl.pallas_call(
        functools.partial(prep_body, devices, radices),
        out_shape=(
            shape((stages, (2 * deepest + 1) * rank, most * rank), BF16),
            shape((stages, 2, (deepest + 1) * rank, most * rank), BF16),
            shape((stages, deepest * rank, rank), F32),
        ),
        grid_spec=pltpu.PrefetchScalarGridSpec(
            num_scalar_prefetch=1,
            grid=(1,),
            in_specs=specs,
            out_specs=(whole, whole, whole),
            scratch_shapes=[pltpu.VMEM((2 * most * rank, most * rank), F32)] * 2,
        ),
        cost_estimate=pl.CostEstimate(flops=int(1e9), bytes_accessed=1 << 20, transcendentals=0),
        compiler_params=pltpu.CompilerParams(vmem_limit_bytes=VMEM_LIMIT),
        name="prep",
    )(me, upper_pick, local_transfer, *([upper_transfer] * (len(specs) - 2)))

    far = call(
        functools.partial(far_body, leaves, rank, cols), shape((leaves * rank, 128), F32), flops=1e9, name="far"
    )(points, weights, local_transfer)
    halves = [
        call(
            functools.partial(leaf_body, first, leaves // 2, rank), shape((items // 2, 256), BF16), flops=2e9, name="leaf"
        )(order, embeddings, rhs_tree, leaf_basis, far)
        for first in (0, leaves // 2)
    ]
    spread = call(
        functools.partial(spread_body, 256), shape((items, 256), BF16), flops=2e9, name="spread"
    )(order, *halves)

    field = None
    base = 0
    for stage, (n, depth) in enumerate(zip(radices, depths)):
        stride = 1 << base
        groups = [
            [high * stride * n + low + stride * j for j in range(n)]
            for high in range(devices // (stride * n))
            for low in range(stride)
        ]
        gathered = lax.all_to_all(payload, "leaf", 0, 0, axis_index_groups=groups)
        base += depth
        if stage + 1 < stages:
            payload, pairs, siblings = call(
                functools.partial(hop_body, stage, depth, rank, cols),
                (
                    shape((radices[stage + 1], rank, width + 2 * cols), BF16),
                    shape((2 * depth * rank, width), BF16),
                    shape((depth * rank, cols), F32),
                ),
                name="hop",
            )(gathered, selects, lifts)
            if field is None:
                body = lambda a, b, c, o, stage=stage, depth=depth: terms_body(stage, depth, rank, a, b, c, None, o)
                field = call(body, shape((rank, cols), F32), name="terms")(pairs, siblings, chains)
            else:
                field = call(functools.partial(terms_body, stage, depth, rank), shape((rank, cols), F32), name="terms")(
                    pairs, siblings, chains, field
                )
    return call(
        functools.partial(final_body, stages - 1, depths[-1], rank, cols), shape((items, cols), BF16), name="final"
    )(gathered, selects, lifts, chains, field, spread)


def solution(mesh):
    return jax.shard_map(
        local,
        mesh=mesh,
        in_specs=(
            P("leaf", None),
            P("leaf", None),
            P("leaf"),
            P("leaf", None),
            P("leaf", None),
            P("leaf", None, None),
            P("leaf", None),
            P(),
            P(),
        ),
        out_specs=P("leaf", None),
        check_vma=False,
    )
```

```python
import functools

import jax
import jax.numpy as jnp
from jax import lax
from jax.experimental import pallas as pl
from jax.experimental.pallas import tpu as pltpu
from jax.sharding import PartitionSpec as P

RIDGE = 1.0
RADICES = {512: (8, 4, 8)}
F32 = jnp.float32
BF16 = jnp.bfloat16
ALL_VMEM = 63 * 1024 * 1024
VMEM_LIMIT = 8 * 1024 * 1024


def dot(a, b):
    return jnp.dot(a, b, preferred_element_type=F32)


def dot_first(a, b):
    return lax.dot_general(a, b, (((0,), (0,)), ((), ())), preferred_element_type=F32)


def dot_last(a, b):
    return lax.dot_general(a, b, (((1,), (1,)), ((), ())), preferred_element_type=F32)


def split(x):
    high = x.astype(BF16)
    return high, (x - high.astype(F32)).astype(BF16)


def dot_wide(a, b):
    a_high, a_low = split(a)
    b_high, b_low = split(b)
    return dot(a_high, b_high) + dot(a_low, b_high) + dot(a_high, b_low)


def dot_right(a, b):
    high, low = split(b)
    return dot(a, high) + dot(a, low)


def dot_first_right(a, b):
    high, low = split(b)
    return dot_first(a, high) + dot_first(a, low)


def dot_first_wide(a, b):
    a_high, a_low = split(a)
    b_high, b_low = split(b)
    return dot_first(a_high, b_high) + dot_first(a_low, b_high) + dot_first(a_high, b_low)


def iota(shape, axis):
    return lax.broadcasted_iota(jnp.int32, shape, axis)


def one_hot(mask):
    return jnp.where(mask, 1.0, 0.0).astype(BF16)


def kernel_of(distance, width):
    return lax.rsqrt(1.0 + jnp.maximum(distance, 0.0) * (1.0 / width))


def self_kernel(points):
    count, width = points.shape
    gram = dot_last(points, points)
    eye = iota(gram.shape, 0) == iota(gram.shape, 1)
    diagonal = jnp.where(eye, gram, 0.0)
    across = jnp.sum(diagonal, axis=1, keepdims=True)
    down = jnp.sum(diagonal, axis=0, keepdims=True)
    return kernel_of(across + down - 2.0 * gram, width), eye


def columns_of(table):
    return table.astype(F32).T.astype(jnp.int32)


def order_column(order_t, leaf):
    return jnp.concatenate([order_t[:, 2 * leaf : 2 * leaf + 1], order_t[:, 2 * leaf + 1 : 2 * leaf + 2]], axis=0)


def order_row(order, leaf):
    return jnp.concatenate([order[2 * leaf : 2 * leaf + 1, :], order[2 * leaf + 1 : 2 * leaf + 2, :]], axis=1)


def padded_columns(tables, rows):
    stacked = jnp.concatenate(tables, axis=0)
    short = rows - stacked.shape[0]
    if short:
        stacked = jnp.concatenate([stacked, jnp.zeros((short, stacked.shape[1]), jnp.int32)], axis=0)
    wide = jnp.concatenate([stacked, jnp.zeros((rows, 128 - stacked.shape[1]), jnp.int32)], axis=1)
    return columns_of(wide)


def fetch(sources, targets, sems):
    copies = [pltpu.make_async_copy(s, t, sems.at[i]) for i, (s, t) in enumerate(zip(sources, targets))]
    for copy in copies:
        copy.start()
    return copies


def digits_of(places, leaf):
    return (places // leaf).astype(F32).astype(BF16), (places & (leaf - 1)).astype(F32).astype(BF16)


def skeleton_ids(leaves, leaf, order, table, rank):
    rows = jnp.concatenate([order[pl.ds(0, leaves, stride=2), :], order[pl.ds(1, leaves, stride=2), :]], axis=1)
    high, low = digits_of(rows, leaf)
    digits = jnp.concatenate([high.astype(F32), low.astype(F32)], axis=0).astype(BF16)
    spots = jnp.concatenate([table[:rank, l : l + 1] for l in range(leaves)], axis=0)
    found = dot_last(one_hot(spots == iota((spots.shape[0], leaf), 1)), digits)
    lane = iota(found.shape, 1)
    own = iota(found.shape, 0) // rank
    block = jnp.sum(jnp.where(lane == own, found, 0.0), axis=1, keepdims=True)
    offset = jnp.sum(jnp.where(lane == own + leaves, found, 0.0), axis=1, keepdims=True)
    lane = iota((spots.shape[0], 128), 1)
    return jnp.where(lane == 0, block, jnp.where(lane == 1, offset, 0.0)).astype(BF16)


def items_of(ids, leaf, emb):
    ids = ids.astype(F32).astype(jnp.int32)
    spots = ids[:, :1] * leaf + ids[:, 1:2]
    return dot(one_hot(spots == iota((ids.shape[0], emb.shape[0]), 1)), emb[...]).astype(BF16)


def picked_of(nodes, parents, table, leaves, rank):
    rows = jnp.concatenate(
        [table[:rank, leaves + q - 1 : leaves + q] + 2 * rank * (q - parents) for q in range(parents, 2 * parents)], axis=0
    )
    return dot(one_hot(rows == iota((parents * rank, nodes.shape[0]), 1)), nodes).astype(BF16)


def pre_body(leaves, *refs):
    sources, (payload, rhs_tree, weights), targets, sems = refs[:7], refs[7:10], refs[10:17], refs[17]
    copies = fetch(sources, targets, sems)
    order, skel, pick, rhs, basis, transfer, emb = targets
    cols, items = rhs.shape
    leaf = items // leaves
    rank = skel.shape[1]
    blocks = items // leaf
    for copy in copies[:3]:
        copy.wait()
    table = padded_columns([skel[...], pick[...]], 16)
    nodes = skeleton_ids(leaves, leaf, order, table, rank)
    parents = leaves // 2
    while parents:
        nodes = picked_of(nodes, parents, table, leaves, rank)
        parents //= 2
    for copy in copies[3:6]:
        copy.wait()
    joined = jnp.concatenate([rhs[:, b * leaf : (b + 1) * leaf] for b in range(blocks)], axis=0)
    level = []
    for l in range(leaves):
        row = order_row(order, l)
        low, high = row & (leaf - 1), row // leaf
        found = dot(joined, one_hot(low == iota((leaf, leaf), 0)))
        total = None
        for b in range(blocks):
            part = jnp.where(high == b, found[b * cols : (b + 1) * cols, :], 0.0)
            total = part if total is None else total + part
        picked = total.astype(BF16)
        rhs_tree[:, l * leaf : (l + 1) * leaf] = picked
        level.append(dot_last(basis[:, l * leaf : (l + 1) * leaf], picked))
    chain = [transfer[1].astype(F32), transfer[2].astype(F32)]
    count = 4
    while count <= leaves:
        chain = [dot_right(transfer[count + n - 1], chain[n // 2]) for n in range(count)]
        count *= 2
    chain = jnp.concatenate(chain, axis=0)
    high, low = split(chain)
    chain = jnp.concatenate([chain, dot(high, transfer[0]) + dot(low, transfer[0])], axis=1)
    level = jnp.concatenate(level, axis=0)
    weights[...] = level
    top = dot_first_wide(chain, level)
    copies[6].wait()
    nodes = items_of(nodes, leaf, emb)
    payload[...] = jnp.concatenate([nodes, top[:rank, :].astype(BF16), top[rank:, :].astype(BF16)], axis=1)


def packed(weights, width):
    rank, cols = weights.shape
    rows = rank * cols // width
    return jnp.concatenate([weights[r : r + rows, :] for r in range(0, rank, rows)], axis=1)


def send(payload, points, weights):
    rank, width = points.shape
    points = points.astype(BF16)
    tail = packed(weights, width).astype(BF16)
    for r in range(payload.shape[0]):
        payload[r, :rank, :] = points
        payload[r, rank:, :] = tail


def side_body(rank, me_ref, mine, pick, hot, kept):
    me = me_ref[0]
    devices = pick.shape[1]
    parent = one_hot(iota((8, devices), 1) == (devices + me) // 2)
    spots = dot_last(pick[...].astype(F32).astype(BF16), parent)[:, :1].astype(jnp.int32)
    shift = jnp.where(me % 2 == 0, 0, rank)
    spots = jnp.where(spots >= shift, spots - shift, spots + rank)
    hot[...] = one_hot(spots == iota((rank, 2 * rank), 1))
    kept[...] = mine[...]


def pair_body(rank, cols, hot, mine, other, payload, pairs, siblings):
    width = mine.shape[1] - 2 * cols
    both = jnp.concatenate([mine[:, :width], other[:, :width]], axis=0)
    pairs[...] = both
    siblings[...] = other[:, width : width + cols].astype(F32)
    total = mine[:, width + cols :].astype(F32) + other[:, width + cols :].astype(F32)
    send(payload, dot(hot[...], both), total)


def slots_of(radix):
    starts, at = [], 0
    for h in range(radix.bit_length()):
        starts.append(at)
        at += radix >> h
    return starts


def prep_body(devices, radices, me_ref, pick_hbm, upper_hbm, local_hbm, *refs):
    selects, lifts, chains, select_all, lift_all, pick, upper, own_transfer, rows_of, sems = refs
    copies = fetch((pick_hbm, upper_hbm, local_hbm.at[pl.ds(0, 1)]), (pick, upper, own_transfer), sems)
    rank = own_transfer.shape[1]
    me = me_ref[0]
    most = max(radices)
    slots = 2 * most
    nodes = slots * len(radices)
    here = iota((nodes, devices), 0)
    wanted = jnp.full((nodes, devices), -1, jnp.int32)
    base = 1
    for stage, radix in enumerate(radices):
        depth = radix.bit_length() - 1
        top = (devices + me) // (1 << (base + depth))
        for h, start in enumerate(slots_of(radix)):
            first = stage * slots + start
            inside = (here >= first) & (here < first + (radix >> h))
            wanted = jnp.where(inside, here - first + top * (radix >> h), wanted)
        base += depth
    hot = one_hot(wanted == iota((nodes, devices), 1))
    for copy in copies:
        copy.wait()
    table = dot_last(pick[...].astype(F32).astype(BF16), hot).astype(jnp.int32)
    flat = dot_last(hot, upper[...].reshape(rank * rank, devices))
    for a in range(rank):
        rows_of[a * nodes : (a + 1) * nodes, :] = flat[:, a * rank : (a + 1) * rank]

    def moved_of(slot):
        return rows_of[pl.ds(slot, rank, stride=nodes), :]

    base = 1
    chain = own_transfer[0].astype(F32)
    for stage, radix in enumerate(radices):
        depth = radix.bit_length() - 1
        place = (me // (1 << base)) % radix
        wide = radix * rank
        starts = [rank * s for s in slots_of(radix)]
        eye = iota((wide, wide), 0) == iota((wide, wide), 1)
        select_all[0:wide, :wide] = jnp.where(eye, 1.0, 0.0)
        lift_all[0:wide, :wide] = jnp.where(eye, 1.0, 0.0)
        for h in range(1, depth + 1):
            below, at = starts[h - 1], starts[h]
            for p in range(radix >> h):
                pair = slice(below + 2 * rank * p, below + 2 * rank * (p + 1))
                spot = slice(at + rank * p, at + rank * (p + 1))
                slot = stage * slots + at // rank + p
                picked = one_hot(table[:, slot : slot + 1] == iota((rank, 2 * rank), 1))
                select_all[spot, :wide] = dot(picked, select_all[pair, :wide].astype(BF16))
                child = stage * slots + below // rank + 2 * p
                moved = jnp.concatenate([moved_of(child), moved_of(child + 1)], axis=0).astype(BF16)
                lift_all[spot, :wide] = dot_first_right(moved, lift_all[pair, :wide])
        steps = [place // (1 << h) for h in range(depth)]
        mine = [pl.multiple_of(starts[h] + rank * s, rank) for h, s in enumerate(steps)]
        others = [pl.multiple_of(starts[h] + rank * (s + 1 - 2 * (s % 2)), rank) for h, s in enumerate(steps)]
        for i, spot in enumerate(mine + others + [starts[depth]]):
            selects[stage, i * rank : (i + 1) * rank, :wide] = select_all[pl.ds(spot, rank), :wide].astype(BF16)
        for i, spot in enumerate(others + [starts[depth]]):
            high, low = split(lift_all[pl.ds(spot, rank), :wide])
            lifts[stage, 0, i * rank : (i + 1) * rank, :wide] = high
            lifts[stage, 1, i * rank : (i + 1) * rank, :wide] = low
        for h in range(depth):
            step = moved_of(stage * slots + starts[h] // rank + steps[h]).astype(BF16)
            chains[stage, h * rank : (h + 1) * rank, :] = chain
            high, low = split(chain)
            chain = dot(high, step) + dot(low, step)
        base += depth


def gathered_nodes(rank, cols, gathered, select, lift):
    count, rows, width = gathered.shape
    wide = count * rank
    points = dot(select[:, :wide], gathered[:, :rank, :].reshape(wide, width)).astype(BF16)
    tails = gathered[:, rank:, :].astype(F32)
    parts = [tails[j, :, c : c + cols] for j in range(count) for c in range(0, width, cols)]
    weights = jnp.concatenate(parts, axis=0).astype(BF16)
    return points, dot(lift[0, :, :wide], weights) + dot(lift[1, :, :wide], weights)


def terms_of(own, other, weights, rank):
    count, width = own.shape
    gram = dot_last(own, other)
    own_wide, other_wide = own.astype(F32), other.astype(F32)
    across = jnp.sum(own_wide * own_wide, axis=1, keepdims=True)
    down = jnp.sum(other_wide * other_wide, axis=1, keepdims=True)
    down = jnp.broadcast_to(down, (count, 128)).T[0:1, :]
    kernel = kernel_of(across + down - 2.0 * gram, width)
    same = iota(gram.shape, 0) // rank == iota(gram.shape, 1) // rank
    return dot_wide(jnp.where(same, kernel, 0.0), weights)


def chained(chain, terms, rank):
    total = None
    for h in range(terms.shape[0] // rank):
        part = dot_wide(chain[h * rank : (h + 1) * rank, :], terms[h * rank : (h + 1) * rank, :])
        total = part if total is None else total + part
    return total


def hop_body(stage, depth, rank, cols, gathered, selects, lifts, payload, pairs, siblings):
    rows = depth * rank
    points, lifted = gathered_nodes(
        rank, cols, gathered, selects[stage, : (2 * depth + 1) * rank, :], lifts[stage, :, : rows + rank, :]
    )
    pairs[...] = points[: 2 * rows, :]
    siblings[...] = lifted[:rows, :]
    send(payload, points[2 * rows :, :], lifted[rows:, :])


def terms_body(depths, rank, chains, *refs):
    total = terms_of(refs[0][:rank, :], refs[0][rank:, :], refs[1][...], rank)
    for stage, depth in enumerate(depths):
        pairs, siblings = refs[2 * stage + 2], refs[2 * stage + 3]
        rows = depth * rank
        terms = terms_of(pairs[:rows, :], pairs[rows:, :], siblings[...], rank)
        total = total + chained(chains[stage], terms, rank)
    refs[-1][...] = total


def final_body(stage, depth, rank, cols, gathered, selects, lifts, chains, before, spread, product):
    rows = depth * rank
    points, lifted = gathered_nodes(
        rank, cols, gathered, selects[stage, : 2 * rows, :], lifts[stage, :, :rows, :]
    )
    terms = terms_of(points[:rows, :], points[rows:, :], lifted, rank)
    field = chained(chains[stage], terms, rank) + before[...]
    high = field.astype(BF16).astype(F32)
    low = field - high
    eye = jnp.where(iota((cols, cols), 0) == iota((cols, cols), 1), 1.0, 0.0)
    right = jnp.concatenate([eye, eye, high, high, low, jnp.zeros_like(low)], axis=0).astype(BF16)
    product[...] = dot_first(right, spread[...]).astype(BF16)


def far_body(leaves, parts, rank, cols, pick, weights, transfer, *refs):
    count = leaves
    terms = []
    table = padded_columns([pick[...]], 8)
    points = jnp.concatenate([ref[...] for ref in refs[:parts]], axis=0)
    result = refs[parts]
    level = weights[...]
    while count > 1:
        kernel, _ = self_kernel(points)
        here = iota(kernel.shape, 0) // rank
        there = iota(kernel.shape, 1) // rank
        partner = here + 1 - 2 * (here % 2)
        terms.append(dot_wide(jnp.where(there == partner, kernel, 0.0), level))
        half = count // 2
        if half > 1:
            points = picked_of(points, half, table, 0, rank)
            level = jnp.concatenate(
                [
                    dot_first_right(
                        transfer[2 * q - 1 : 2 * q + 1].reshape(2 * rank, rank),
                        level[2 * rank * (q - half) : 2 * rank * (q - half + 1), :],
                    )
                    for q in range(half, 2 * half)
                ],
                axis=0,
            )
        count = half
    below = None
    for height in reversed(range(len(terms))):
        count = leaves >> height
        nodes = []
        for n in range(count):
            moved = transfer[count + n - 1]
            term = terms[height][n * rank : (n + 1) * rank, :]
            if below is None:
                node = jnp.concatenate([term, moved.astype(F32), jnp.zeros((rank, 128 - cols - rank), F32)], axis=1)
            else:
                pad = jnp.zeros((rank, 128 - cols), F32)
                node = dot_right(moved, below[n // 2]) + jnp.concatenate([term, pad], axis=1)
            nodes.append(node)
        below = nodes
    result[...] = jnp.concatenate(below, axis=0)


def leaf_body(first, count, rank, order, emb, rhs_tree, skel, near, points):
    items = emb.shape[0]
    leaf = near.shape[1] // count
    order_t = columns_of(order[...])
    table = padded_columns([skel[...]], 8)
    for i in range(0, count, 2):
        column = jnp.concatenate([order_column(order_t, first + i), order_column(order_t, first + i + 1)], axis=0)
        high, low = digits_of(column, leaf)
        offset = one_hot(iota((2 * leaf, leaf), 1) == (column & (leaf - 1)))
        block = jnp.broadcast_to(high, (2 * leaf, leaf))
        hot = jnp.concatenate([jnp.where(block == b, offset, jnp.zeros_like(offset)) for b in range(items // leaf)], axis=1)
        both = dot(hot, emb[...]).astype(BF16)
        for j in range(i, i + 2):
            l = first + j
            feats = both[(j - i) * leaf : (j - i + 1) * leaf, :]
            kernel, eye = self_kernel(feats)
            kernel = jnp.where(eye, kernel + RIDGE, kernel).astype(BF16)
            near[:, j * leaf : (j + 1) * leaf] = dot(rhs_tree[:, l * leaf : (l + 1) * leaf], kernel)
            spots = one_hot(table[:rank, l : l + 1] == iota((rank, leaf), 1))
            points[j * rank : (j + 1) * rank, :] = dot(spots, feats).astype(BF16)


def spread_body(parts, leaf, rank, order, basis, far, *refs):
    near, result, tree, offset, block = refs[:parts], refs[parts], refs[parts + 1], refs[parts + 2], refs[parts + 3]
    items = basis.shape[1]
    cols = near[0].shape[0]
    order_t = columns_of(order[...])
    for c in range(order.shape[0]):
        column = order_t[:, c : c + 1]
        rows = slice(c * 128, (c + 1) * 128)
        offset[rows, :] = one_hot(iota((128, leaf), 1) == (column & (leaf - 1)))
        block[rows, :] = jnp.broadcast_to(digits_of(column, leaf)[0], (128, leaf))
    l = 0
    for part in near:
        for i in range(part.shape[1] // leaf):
            lanes = slice(l * leaf, (l + 1) * leaf)
            high, low = split(far[l * rank : (l + 1) * rank, :])
            both = dot_first(high, basis[:, lanes]) + dot_first(low, basis[:, lanes])
            total = part[:, i * leaf : (i + 1) * leaf] + both[:cols, :]
            total_high = total.astype(BF16).astype(F32)
            moved = both[cols : cols + rank, :]
            moved_high = moved.astype(BF16).astype(F32)
            tree[:, lanes] = jnp.concatenate(
                [total_high, total - total_high, moved_high, moved - moved_high, moved_high, jnp.zeros_like(moved)], axis=0
            ).astype(BF16)
            l += 1
    for b in range(items // leaf):
        hot = jnp.where(block[...] == b, offset[...], jnp.zeros_like(offset))
        result[:, b * leaf : (b + 1) * leaf] = dot(tree[...], hot).astype(BF16)


def call(body, outs, scratch=(), flops=1e8, name=None, specs=None, limit=VMEM_LIMIT):
    extra = {} if specs is None else {"in_specs": specs}
    return pl.pallas_call(
        body,
        out_shape=outs,
        scratch_shapes=list(scratch),
        cost_estimate=pl.CostEstimate(flops=int(flops), bytes_accessed=1 << 20, transcendentals=0),
        compiler_params=pltpu.CompilerParams(vmem_limit_bytes=limit),
        name=name,
        **extra,
    )


def after(values, earlier):
    return lax.optimization_barrier((*values, earlier))[:-1]


def shape(dims, dtype):
    return jax.ShapeDtypeStruct(dims, dtype)


def local(
    embeddings,
    rhs,
    item_order,
    leaf_basis,
    leaf_skel,
    local_transfer,
    local_pick,
    upper_transfer,
    upper_pick,
):
    leaves, rank = leaf_skel.shape
    items, cols = rhs.shape
    width = embeddings.shape[1]
    devices = lax.axis_size("leaf")
    radices = RADICES[devices]
    me = lax.axis_index("leaf")
    me = me.astype(jnp.int32).reshape(1)
    order = item_order.reshape(items // 128, 128)
    basis_t = leaf_basis.T
    far_away = pl.BlockSpec(memory_space=pltpu.HBM)

    given = (order, leaf_skel, local_pick, rhs.T, basis_t, local_transfer, embeddings)
    payload, rhs_tree, weights = call(
        functools.partial(pre_body, leaves),
        (
            shape((rank, width + 2 * cols), BF16),
            shape((cols, items), BF16),
            shape((leaves * rank, cols), F32),
        ),
        scratch=[pltpu.VMEM(x.shape, x.dtype) for x in given] + [pltpu.SemaphoreType.DMA((len(given),))],
        specs=[far_away] * len(given),
        limit=ALL_VMEM,
        name="pre",
    )(*given)
    other = lax.ppermute(payload, "leaf", [(i, i ^ 1) for i in range(devices)])
    memory = pl.BlockSpec(memory_space=pltpu.SMEM)
    whole = pl.BlockSpec(memory_space=pltpu.VMEM)
    hot, kept = call(
        functools.partial(side_body, rank),
        (shape((rank, 2 * rank), BF16), shape(payload.shape, BF16)),
        specs=[memory] + [whole] * 2,
        name="side",
    )(me, payload, upper_pick.T)
    sent = rank + rank * cols // width
    payload, pairs, siblings = call(
        functools.partial(pair_body, rank, cols),
        (
            shape((radices[0], sent, width), BF16),
            shape((2 * rank, width), BF16),
            shape((rank, cols), F32),
        ),
        name="pair",
    )(hot, kept, other)
    held = [pairs, siblings]

    stages = len(radices)
    most = max(radices)
    depths = [n.bit_length() - 1 for n in radices]
    deepest = max(depths)
    nodes = 2 * most * stages
    (me,) = after((me,), payload)
    selects, lifts, chains = call(
        functools.partial(prep_body, devices, radices),
        (
            shape((stages, (2 * deepest + 1) * rank, most * rank), BF16),
            shape((stages, 2, (deepest + 1) * rank, most * rank), BF16),
            shape((stages, deepest * rank, rank), F32),
        ),
        scratch=[
            pltpu.VMEM((2 * most * rank, most * rank), F32),
            pltpu.VMEM((2 * most * rank, most * rank), F32),
            pltpu.VMEM((rank, devices), jnp.int32),
            pltpu.VMEM((rank, rank, devices), BF16),
            pltpu.VMEM((1, rank, rank), BF16),
            pltpu.VMEM((rank * nodes, rank), F32),
            pltpu.SemaphoreType.DMA((3,)),
        ],
        specs=[memory] + [far_away] * 3,
        flops=2e9,
        name="prep",
    )(me, upper_pick.T, upper_transfer.transpose(1, 2, 0), local_transfer)

    def leaf_part(first, count, earlier):
        return call(
            functools.partial(leaf_body, first, count, rank),
            (shape((cols, items // leaves * count), F32), shape((count * rank, width), BF16)),
            flops=2e9,
            name="leaf",
        )(after((order,), earlier)[0], embeddings, rhs_tree, leaf_skel)

    lead = leaves * 3 // 4
    parts = [leaf_part(0, lead, payload)]
    base = 1
    for stage, (n, depth) in enumerate(zip(radices, depths)):
        stride = 1 << base
        groups = [
            [high * stride * n + low + stride * j for j in range(n)]
            for high in range(devices // (stride * n))
            for low in range(stride)
        ]
        gathered = lax.all_to_all(payload, "leaf", 0, 0, axis_index_groups=groups)
        base += depth
        if stage == 1:
            parts.append(leaf_part(lead, leaves - lead, payload))
            far = call(
                functools.partial(far_body, leaves, len(parts), rank, cols),
                shape((leaves * rank, 128), F32),
                flops=1e9,
                name="far",
            )(local_pick, weights, local_transfer, *[part[1] for part in parts])
            if stage + 1 < stages:
                gathered, far = lax.optimization_barrier((gathered, far))
        elif stage + 1 < stages:
            gathered, parts[-1] = lax.optimization_barrier((gathered, parts[-1]))
        if stage + 1 < stages:
            payload, pairs, siblings = call(
                functools.partial(hop_body, stage, depth, rank, cols),
                (
                    shape((radices[stage + 1], sent, width), BF16),
                    shape((2 * depth * rank, width), BF16),
                    shape((depth * rank, cols), F32),
                ),
                name="hop",
            )(gathered, selects, lifts)
            held += [pairs, siblings]
    chains_last, far = after((chains, far), payload)
    spread = call(
        functools.partial(spread_body, len(parts), items // leaves, rank),
        shape((256, items), BF16),
        scratch=[
            pltpu.VMEM((256, items), BF16),
            pltpu.VMEM((items, items // leaves), BF16),
            pltpu.VMEM((items, items // leaves), BF16),
        ],
        flops=2e9,
        name="spread",
    )(order, basis_t, far, *[part[0] for part in parts])
    field = call(functools.partial(terms_body, depths[:-1], rank), shape((rank, cols), F32), name="terms")(chains_last, *held)
    product = call(
        functools.partial(final_body, stages - 1, depths[-1], rank, cols), shape((cols, items), BF16), name="final"
    )(gathered, selects, lifts, chains, field, spread)
    return product.T


def solution(mesh):
    return jax.shard_map(
        local,
        mesh=mesh,
        in_specs=(
            P("leaf", None),
            P("leaf", None),
            P("leaf"),
            P("leaf", None),
            P("leaf", None),
            P("leaf", None, None),
            P("leaf", None),
            P(),
            P(),
        ),
        out_specs=P("leaf", None),
        check_vma=False,
    )
```

```python
import functools

import jax
import jax.numpy as jnp
from jax import lax
from jax.experimental import pallas as pl
from jax.experimental.pallas import tpu as pltpu
from jax.sharding import PartitionSpec as P

RIDGE = 1.0
RADICES = {512: (8, 4, 8)}
F32 = jnp.float32
BF16 = jnp.bfloat16
ALL_VMEM = 63 * 1024 * 1024
VMEM_LIMIT = 8 * 1024 * 1024


def dot(a, b):
    return jnp.dot(a, b, preferred_element_type=F32)


def dot_first(a, b):
    return lax.dot_general(a, b, (((0,), (0,)), ((), ())), preferred_element_type=F32)


def dot_last(a, b):
    return lax.dot_general(a, b, (((1,), (1,)), ((), ())), preferred_element_type=F32)


def split(x):
    high = x.astype(BF16)
    return high, (x - high.astype(F32)).astype(BF16)


def dot_wide(a, b):
    a_high, a_low = split(a)
    b_high, b_low = split(b)
    return dot(a_high, b_high) + dot(a_low, b_high) + dot(a_high, b_low)


def dot_right(a, b):
    high, low = split(b)
    return dot(a, high) + dot(a, low)


def dot_first_right(a, b):
    high, low = split(b)
    return dot_first(a, high) + dot_first(a, low)


def dot_first_wide(a, b):
    a_high, a_low = split(a)
    b_high, b_low = split(b)
    return dot_first(a_high, b_high) + dot_first(a_low, b_high) + dot_first(a_high, b_low)


def iota(shape, axis):
    return lax.broadcasted_iota(jnp.int32, shape, axis)


def one_hot(mask):
    return jnp.where(mask, 1.0, 0.0).astype(BF16)


def kernel_of(distance, width):
    return lax.rsqrt(1.0 + jnp.maximum(distance, 0.0) * (1.0 / width))


def self_kernel(points):
    count, width = points.shape
    gram = dot_last(points, points)
    eye = iota(gram.shape, 0) == iota(gram.shape, 1)
    diagonal = jnp.where(eye, gram, 0.0)
    across = jnp.sum(diagonal, axis=1, keepdims=True)
    down = jnp.sum(diagonal, axis=0, keepdims=True)
    return kernel_of(across + down - 2.0 * gram, width), eye


def columns_of(table):
    return table.astype(F32).T.astype(jnp.int32)


def order_column(order_t, leaf):
    return jnp.concatenate([order_t[:, 2 * leaf : 2 * leaf + 1], order_t[:, 2 * leaf + 1 : 2 * leaf + 2]], axis=0)


def order_row(order, leaf):
    return jnp.concatenate([order[2 * leaf : 2 * leaf + 1, :], order[2 * leaf + 1 : 2 * leaf + 2, :]], axis=1)


def padded_columns(tables, rows):
    stacked = jnp.concatenate(tables, axis=0)
    short = rows - stacked.shape[0]
    if short:
        stacked = jnp.concatenate([stacked, jnp.zeros((short, stacked.shape[1]), jnp.int32)], axis=0)
    wide = jnp.concatenate([stacked, jnp.zeros((rows, 128 - stacked.shape[1]), jnp.int32)], axis=1)
    return columns_of(wide)


def fetch(sources, targets, sems):
    copies = [pltpu.make_async_copy(s, t, sems.at[i]) for i, (s, t) in enumerate(zip(sources, targets))]
    for copy in copies:
        copy.start()
    return copies


def digits_of(places, leaf):
    return (places // leaf).astype(F32).astype(BF16), (places & (leaf - 1)).astype(F32).astype(BF16)


def skeleton_ids(leaves, leaf, order, table, rank):
    rows = jnp.concatenate([order[pl.ds(0, leaves, stride=2), :], order[pl.ds(1, leaves, stride=2), :]], axis=1)
    high, low = digits_of(rows, leaf)
    digits = jnp.concatenate([high.astype(F32), low.astype(F32)], axis=0).astype(BF16)
    spots = jnp.concatenate([table[:rank, l : l + 1] for l in range(leaves)], axis=0)
    found = dot_last(one_hot(spots == iota((spots.shape[0], leaf), 1)), digits)
    lane = iota(found.shape, 1)
    own = iota(found.shape, 0) // rank
    block = jnp.sum(jnp.where(lane == own, found, 0.0), axis=1, keepdims=True)
    offset = jnp.sum(jnp.where(lane == own + leaves, found, 0.0), axis=1, keepdims=True)
    lane = iota((spots.shape[0], 128), 1)
    return jnp.where(lane == 0, block, jnp.where(lane == 1, offset, 0.0)).astype(BF16)


def items_of(ids, leaf, emb):
    ids = ids.astype(F32).astype(jnp.int32)
    spots = ids[:, :1] * leaf + ids[:, 1:2]
    return dot(one_hot(spots == iota((ids.shape[0], emb.shape[0]), 1)), emb[...]).astype(BF16)


def picked_of(nodes, parents, table, leaves, rank):
    rows = jnp.concatenate(
        [table[:rank, leaves + q - 1 : leaves + q] + 2 * rank * (q - parents) for q in range(parents, 2 * parents)], axis=0
    )
    return dot(one_hot(rows == iota((parents * rank, nodes.shape[0]), 1)), nodes).astype(BF16)


def pre_body(leaves, *refs):
    sources, (payload, rhs_tree, weights), targets, sems = refs[:7], refs[7:10], refs[10:17], refs[17]
    copies = fetch(sources, targets, sems)
    order, skel, pick, rhs, basis, transfer, emb = targets
    cols, items = rhs.shape
    leaf = items // leaves
    rank = skel.shape[1]
    blocks = items // leaf
    for copy in copies[:6]:
        copy.wait()
    table = padded_columns([skel[...], pick[...]], 16)
    joined = jnp.concatenate([rhs[:, b * leaf : (b + 1) * leaf] for b in range(blocks)], axis=0)

    def gather(l):
        row = order_row(order, l)
        low, high = row & (leaf - 1), row // leaf
        found = dot(joined, one_hot(low == iota((leaf, leaf), 0)))
        total = None
        for b in range(blocks):
            part = jnp.where(high == b, found[b * cols : (b + 1) * cols, :], 0.0)
            total = part if total is None else total + part
        picked = total.astype(BF16)
        rhs_tree[:, l * leaf : (l + 1) * leaf] = picked
        lifted = dot_last(basis[:, l * leaf : (l + 1) * leaf], picked)
        weights[l * rank : (l + 1) * rank, :] = lifted
        return lifted

    def lift(q, left, right):
        pair = jnp.concatenate([left, right], axis=0)
        return dot_first_right(transfer[2 * q - 1 : 2 * q + 1].reshape(2 * rank, rank), pair)

    nodes, parents, pending = None, leaves, {}
    for l in range(leaves):
        node, q = gather(l), leaves + l
        if l == 1:
            copies[6].wait()
        if l == leaves - 1:
            nodes = items_of(nodes, leaf, emb)
        while q % 2:
            node = lift(q // 2, pending.pop(q - 1), node)
            q //= 2
            if q == 1:
                break
        pending[q] = node
        if nodes is None:
            nodes = skeleton_ids(leaves, leaf, order, table, rank)
        elif parents > 1:
            parents //= 2
            nodes = picked_of(nodes, parents, table, leaves, rank)
    while parents > 1:
        parents //= 2
        nodes = picked_of(nodes, parents, table, leaves, rank)
    own = pending[1]
    share = dot_first_right(transfer[0], own)
    payload[...] = jnp.concatenate([nodes, own.astype(BF16), share.astype(BF16)], axis=1)


def packed(weights, width):
    rank, cols = weights.shape
    rows = rank * cols // width
    return jnp.concatenate([weights[r : r + rows, :] for r in range(0, rank, rows)], axis=1)


def send(payload, points, weights):
    rank, width = points.shape
    points = points.astype(BF16)
    tail = packed(weights, width).astype(BF16)
    for r in range(payload.shape[0]):
        payload[r, :rank, :] = points
        payload[r, rank:, :] = tail


def side_body(rank, me_ref, mine, pick, hot, kept):
    me = me_ref[0]
    devices = pick.shape[1]
    parent = one_hot(iota((8, devices), 1) == (devices + me) // 2)
    spots = dot_last(pick[...].astype(F32).astype(BF16), parent)[:, :1].astype(jnp.int32)
    shift = jnp.where(me % 2 == 0, 0, rank)
    spots = jnp.where(spots >= shift, spots - shift, spots + rank)
    hot[...] = one_hot(spots == iota((rank, 2 * rank), 1))
    kept[...] = mine[...]


def pair_body(rank, cols, hot, mine, other, payload, pairs, siblings):
    width = mine.shape[1] - 2 * cols
    both = jnp.concatenate([mine[:, :width], other[:, :width]], axis=0)
    pairs[...] = both
    siblings[...] = other[:, width : width + cols].astype(F32)
    total = mine[:, width + cols :].astype(F32) + other[:, width + cols :].astype(F32)
    send(payload, dot(hot[...], both), total)


def slots_of(radix):
    starts, at = [], 0
    for h in range(radix.bit_length()):
        starts.append(at)
        at += radix >> h
    return starts


def prep_body(devices, radices, me_ref, pick_hbm, upper_hbm, local_hbm, *refs):
    selects, lifts, chains, select_all, lift_all, pick, upper, own_transfer, rows_of, sems = refs
    copies = fetch((pick_hbm, upper_hbm, local_hbm.at[pl.ds(0, 1)]), (pick, upper, own_transfer), sems)
    rank = own_transfer.shape[1]
    me = me_ref[0]
    most = max(radices)
    slots = 2 * most
    nodes = slots * len(radices)
    here = iota((nodes, devices), 0)
    wanted = jnp.full((nodes, devices), -1, jnp.int32)
    base = 1
    for stage, radix in enumerate(radices):
        depth = radix.bit_length() - 1
        top = (devices + me) // (1 << (base + depth))
        for h, start in enumerate(slots_of(radix)):
            first = stage * slots + start
            inside = (here >= first) & (here < first + (radix >> h))
            wanted = jnp.where(inside, here - first + top * (radix >> h), wanted)
        base += depth
    hot = one_hot(wanted == iota((nodes, devices), 1))
    for copy in copies:
        copy.wait()
    table = dot_last(pick[...].astype(F32).astype(BF16), hot).astype(jnp.int32)
    flat = dot_last(hot, upper[...].reshape(rank * rank, devices))
    for a in range(rank):
        rows_of[a * nodes : (a + 1) * nodes, :] = flat[:, a * rank : (a + 1) * rank]

    def moved_of(slot):
        return rows_of[pl.ds(slot, rank, stride=nodes), :]

    base = 1
    chain = own_transfer[0].astype(F32)
    for stage, radix in enumerate(radices):
        depth = radix.bit_length() - 1
        place = (me // (1 << base)) % radix
        wide = radix * rank
        starts = [rank * s for s in slots_of(radix)]
        eye = iota((wide, wide), 0) == iota((wide, wide), 1)
        select_all[0:wide, :wide] = jnp.where(eye, 1.0, 0.0)
        lift_all[0:wide, :wide] = jnp.where(eye, 1.0, 0.0)
        for h in range(1, depth + 1):
            below, at = starts[h - 1], starts[h]
            for p in range(radix >> h):
                pair = slice(below + 2 * rank * p, below + 2 * rank * (p + 1))
                spot = slice(at + rank * p, at + rank * (p + 1))
                slot = stage * slots + at // rank + p
                picked = one_hot(table[:, slot : slot + 1] == iota((rank, 2 * rank), 1))
                select_all[spot, :wide] = dot(picked, select_all[pair, :wide].astype(BF16))
                child = stage * slots + below // rank + 2 * p
                moved = jnp.concatenate([moved_of(child), moved_of(child + 1)], axis=0).astype(BF16)
                lift_all[spot, :wide] = dot_first_right(moved, lift_all[pair, :wide])
        steps = [place // (1 << h) for h in range(depth)]
        mine = [pl.multiple_of(starts[h] + rank * s, rank) for h, s in enumerate(steps)]
        others = [pl.multiple_of(starts[h] + rank * (s + 1 - 2 * (s % 2)), rank) for h, s in enumerate(steps)]
        for i, spot in enumerate(mine + others + [starts[depth]]):
            selects[stage, i * rank : (i + 1) * rank, :wide] = select_all[pl.ds(spot, rank), :wide].astype(BF16)
        for i, spot in enumerate(others + [starts[depth]]):
            high, low = split(lift_all[pl.ds(spot, rank), :wide])
            lifts[stage, 0, i * rank : (i + 1) * rank, :wide] = high
            lifts[stage, 1, i * rank : (i + 1) * rank, :wide] = low
        for h in range(depth):
            step = moved_of(stage * slots + starts[h] // rank + steps[h]).astype(BF16)
            chains[stage, h * rank : (h + 1) * rank, :] = chain
            high, low = split(chain)
            chain = dot(high, step) + dot(low, step)
        base += depth


def gathered_nodes(rank, cols, gathered, select, lift):
    count, rows, width = gathered.shape
    wide = count * rank
    points = dot(select[:, :wide], gathered[:, :rank, :].reshape(wide, width)).astype(BF16)
    tails = gathered[:, rank:, :].astype(F32)
    parts = [tails[j, :, c : c + cols] for j in range(count) for c in range(0, width, cols)]
    weights = jnp.concatenate(parts, axis=0).astype(BF16)
    return points, dot(lift[0, :, :wide], weights) + dot(lift[1, :, :wide], weights)


def terms_of(own, other, weights, rank):
    count, width = own.shape
    gram = dot_last(own, other)
    own_wide, other_wide = own.astype(F32), other.astype(F32)
    across = jnp.sum(own_wide * own_wide, axis=1, keepdims=True)
    down = jnp.sum(other_wide * other_wide, axis=1, keepdims=True)
    down = jnp.broadcast_to(down, (count, 128)).T[0:1, :]
    kernel = kernel_of(across + down - 2.0 * gram, width)
    same = iota(gram.shape, 0) // rank == iota(gram.shape, 1) // rank
    return dot_wide(jnp.where(same, kernel, 0.0), weights)


def chained(chain, terms, rank):
    total = None
    for h in range(terms.shape[0] // rank):
        part = dot_wide(chain[h * rank : (h + 1) * rank, :], terms[h * rank : (h + 1) * rank, :])
        total = part if total is None else total + part
    return total


def hop_body(stage, depth, rank, cols, gathered, selects, lifts, payload, pairs, siblings):
    rows = depth * rank
    points, lifted = gathered_nodes(
        rank, cols, gathered, selects[stage, : (2 * depth + 1) * rank, :], lifts[stage, :, : rows + rank, :]
    )
    pairs[...] = points[: 2 * rows, :]
    siblings[...] = lifted[:rows, :]
    send(payload, points[2 * rows :, :], lifted[rows:, :])


def terms_body(depths, rank, chains, *refs):
    total = terms_of(refs[0][:rank, :], refs[0][rank:, :], refs[1][...], rank)
    for stage, depth in enumerate(depths):
        pairs, siblings = refs[2 * stage + 2], refs[2 * stage + 3]
        rows = depth * rank
        terms = terms_of(pairs[:rows, :], pairs[rows:, :], siblings[...], rank)
        total = total + chained(chains[stage], terms, rank)
    refs[-1][...] = total


def final_body(stage, depth, rank, cols, gathered, selects, lifts, chains, before, spread, product):
    rows = depth * rank
    points, lifted = gathered_nodes(
        rank, cols, gathered, selects[stage, : 2 * rows, :], lifts[stage, :, :rows, :]
    )
    terms = terms_of(points[:rows, :], points[rows:, :], lifted, rank)
    field = chained(chains[stage], terms, rank) + before[...]
    high = field.astype(BF16).astype(F32)
    low = field - high
    eye = jnp.where(iota((cols, cols), 0) == iota((cols, cols), 1), 1.0, 0.0)
    right = jnp.concatenate([eye, eye, high, high, low, jnp.zeros_like(low)], axis=0).astype(BF16)
    product[...] = dot_first(right, spread[...]).astype(BF16)


def far_body(leaves, parts, rank, cols, pick, weights, transfer, *refs):
    count = leaves
    terms = []
    table = padded_columns([pick[...]], 8)
    points = jnp.concatenate([ref[...] for ref in refs[:parts]], axis=0)
    result = refs[parts]
    level = weights[...]
    while count > 1:
        kernel, _ = self_kernel(points)
        here = iota(kernel.shape, 0) // rank
        there = iota(kernel.shape, 1) // rank
        partner = here + 1 - 2 * (here % 2)
        terms.append(dot_wide(jnp.where(there == partner, kernel, 0.0), level))
        half = count // 2
        if half > 1:
            points = picked_of(points, half, table, 0, rank)
            level = jnp.concatenate(
                [
                    dot_first_right(
                        transfer[2 * q - 1 : 2 * q + 1].reshape(2 * rank, rank),
                        level[2 * rank * (q - half) : 2 * rank * (q - half + 1), :],
                    )
                    for q in range(half, 2 * half)
                ],
                axis=0,
            )
        count = half
    below = None
    for height in reversed(range(len(terms))):
        count = leaves >> height
        nodes = []
        for n in range(count):
            moved = transfer[count + n - 1]
            term = terms[height][n * rank : (n + 1) * rank, :]
            if below is None:
                node = jnp.concatenate([term, moved.astype(F32), jnp.zeros((rank, 128 - cols - rank), F32)], axis=1)
            else:
                pad = jnp.zeros((rank, 128 - cols), F32)
                node = dot_right(moved, below[n // 2]) + jnp.concatenate([term, pad], axis=1)
            nodes.append(node)
        below = nodes
    result[...] = jnp.concatenate(below, axis=0)


def leaf_body(first, count, rank, order, emb, rhs_tree, skel, near, points):
    items = emb.shape[0]
    leaf = near.shape[1] // count
    order_t = columns_of(order[...])
    table = padded_columns([skel[...]], 8)
    for i in range(0, count, 2):
        column = jnp.concatenate([order_column(order_t, first + i), order_column(order_t, first + i + 1)], axis=0)
        high, low = digits_of(column, leaf)
        offset = one_hot(iota((2 * leaf, leaf), 1) == (column & (leaf - 1)))
        block = jnp.broadcast_to(high, (2 * leaf, leaf))
        hot = jnp.concatenate([jnp.where(block == b, offset, jnp.zeros_like(offset)) for b in range(items // leaf)], axis=1)
        both = dot(hot, emb[...]).astype(BF16)
        for j in range(i, i + 2):
            l = first + j
            feats = both[(j - i) * leaf : (j - i + 1) * leaf, :]
            kernel, eye = self_kernel(feats)
            kernel = jnp.where(eye, kernel + RIDGE, kernel).astype(BF16)
            near[:, j * leaf : (j + 1) * leaf] = dot(rhs_tree[:, l * leaf : (l + 1) * leaf], kernel)
            spots = one_hot(table[:rank, l : l + 1] == iota((rank, leaf), 1))
            points[j * rank : (j + 1) * rank, :] = dot(spots, feats).astype(BF16)


def spread_body(parts, leaf, rank, order, basis, far, *refs):
    near, result, tree, offset, block = refs[:parts], refs[parts], refs[parts + 1], refs[parts + 2], refs[parts + 3]
    items = basis.shape[1]
    cols = near[0].shape[0]
    order_t = columns_of(order[...])
    for c in range(order.shape[0]):
        column = order_t[:, c : c + 1]
        rows = slice(c * 128, (c + 1) * 128)
        offset[rows, :] = one_hot(iota((128, leaf), 1) == (column & (leaf - 1)))
        block[rows, :] = jnp.broadcast_to(digits_of(column, leaf)[0], (128, leaf))
    l = 0
    for part in near:
        for i in range(part.shape[1] // leaf):
            lanes = slice(l * leaf, (l + 1) * leaf)
            high, low = split(far[l * rank : (l + 1) * rank, :])
            both = dot_first(high, basis[:, lanes]) + dot_first(low, basis[:, lanes])
            total = part[:, i * leaf : (i + 1) * leaf] + both[:cols, :]
            total_high = total.astype(BF16).astype(F32)
            moved = both[cols : cols + rank, :]
            moved_high = moved.astype(BF16).astype(F32)
            tree[:, lanes] = jnp.concatenate(
                [total_high, total - total_high, moved_high, moved - moved_high, moved_high, jnp.zeros_like(moved)], axis=0
            ).astype(BF16)
            l += 1
    for b in range(items // leaf):
        hot = jnp.where(block[...] == b, offset[...], jnp.zeros_like(offset))
        result[:, b * leaf : (b + 1) * leaf] = dot(tree[...], hot).astype(BF16)


def call(body, outs, scratch=(), flops=1e8, name=None, specs=None, limit=VMEM_LIMIT):
    extra = {} if specs is None else {"in_specs": specs}
    return pl.pallas_call(
        body,
        out_shape=outs,
        scratch_shapes=list(scratch),
        cost_estimate=pl.CostEstimate(flops=int(flops), bytes_accessed=1 << 20, transcendentals=0),
        compiler_params=pltpu.CompilerParams(vmem_limit_bytes=limit),
        name=name,
        **extra,
    )


def after(values, earlier):
    return lax.optimization_barrier((*values, earlier))[:-1]


def shape(dims, dtype):
    return jax.ShapeDtypeStruct(dims, dtype)


def local(
    embeddings,
    rhs,
    item_order,
    leaf_basis,
    leaf_skel,
    local_transfer,
    local_pick,
    upper_transfer,
    upper_pick,
):
    leaves, rank = leaf_skel.shape
    items, cols = rhs.shape
    width = embeddings.shape[1]
    devices = lax.axis_size("leaf")
    radices = RADICES[devices]
    me = lax.axis_index("leaf")
    me = me.astype(jnp.int32).reshape(1)
    order = item_order.reshape(items // 128, 128)
    basis_t = leaf_basis.T
    far_away = pl.BlockSpec(memory_space=pltpu.HBM)

    given = (order, leaf_skel, local_pick, rhs.T, basis_t, local_transfer, embeddings)
    payload, rhs_tree, weights = call(
        functools.partial(pre_body, leaves),
        (
            shape((rank, width + 2 * cols), BF16),
            shape((cols, items), BF16),
            shape((leaves * rank, cols), F32),
        ),
        scratch=[pltpu.VMEM(x.shape, x.dtype) for x in given] + [pltpu.SemaphoreType.DMA((len(given),))],
        specs=[far_away] * len(given),
        limit=ALL_VMEM,
        name="pre",
    )(*given)
    other = lax.ppermute(payload, "leaf", [(i, i ^ 1) for i in range(devices)])
    memory = pl.BlockSpec(memory_space=pltpu.SMEM)
    whole = pl.BlockSpec(memory_space=pltpu.VMEM)
    hot, kept = call(
        functools.partial(side_body, rank),
        (shape((rank, 2 * rank), BF16), shape(payload.shape, BF16)),
        specs=[memory] + [whole] * 2,
        name="side",
    )(me, payload, upper_pick.T)
    sent = rank + rank * cols // width
    payload, pairs, siblings = call(
        functools.partial(pair_body, rank, cols),
        (
            shape((radices[0], sent, width), BF16),
            shape((2 * rank, width), BF16),
            shape((rank, cols), F32),
        ),
        name="pair",
    )(hot, kept, other)
    held = [pairs, siblings]

    stages = len(radices)
    most = max(radices)
    depths = [n.bit_length() - 1 for n in radices]
    deepest = max(depths)
    nodes = 2 * most * stages
    (me,) = after((me,), payload)
    selects, lifts, chains = call(
        functools.partial(prep_body, devices, radices),
        (
            shape((stages, (2 * deepest + 1) * rank, most * rank), BF16),
            shape((stages, 2, (deepest + 1) * rank, most * rank), BF16),
            shape((stages, deepest * rank, rank), F32),
        ),
        scratch=[
            pltpu.VMEM((2 * most * rank, most * rank), F32),
            pltpu.VMEM((2 * most * rank, most * rank), F32),
            pltpu.VMEM((rank, devices), jnp.int32),
            pltpu.VMEM((rank, rank, devices), BF16),
            pltpu.VMEM((1, rank, rank), BF16),
            pltpu.VMEM((rank * nodes, rank), F32),
            pltpu.SemaphoreType.DMA((3,)),
        ],
        specs=[memory] + [far_away] * 3,
        flops=2e9,
        name="prep",
    )(me, upper_pick.T, upper_transfer.transpose(1, 2, 0), local_transfer)

    def leaf_part(first, count, earlier):
        return call(
            functools.partial(leaf_body, first, count, rank),
            (shape((cols, items // leaves * count), F32), shape((count * rank, width), BF16)),
            flops=2e9,
            name="leaf",
        )(after((order,), earlier)[0], embeddings, rhs_tree, leaf_skel)

    lead = leaves // 2
    parts = [leaf_part(0, lead, chains)]
    base = 1
    for stage, (n, depth) in enumerate(zip(radices, depths)):
        stride = 1 << base
        groups = [
            [high * stride * n + low + stride * j for j in range(n)]
            for high in range(devices // (stride * n))
            for low in range(stride)
        ]
        gathered = lax.all_to_all(payload, "leaf", 0, 0, axis_index_groups=groups)
        base += depth
        if stage == 1:
            parts.append(leaf_part(lead, leaves - lead, payload))
        if stage + 1 < stages:
            gathered, *held_points = lax.optimization_barrier((gathered, *parts[-1]))
            parts[-1] = held_points
        if stage + 1 < stages:
            payload, pairs, siblings = call(
                functools.partial(hop_body, stage, depth, rank, cols),
                (
                    shape((radices[stage + 1], sent, width), BF16),
                    shape((2 * depth * rank, width), BF16),
                    shape((depth * rank, cols), F32),
                ),
                name="hop",
            )(gathered, selects, lifts)
            held += [pairs, siblings]
    chains_last, far_weights = after((chains, weights), payload)
    far = call(
        functools.partial(far_body, leaves, len(parts), rank, cols),
        shape((leaves * rank, 128), F32),
        flops=1e9,
        name="far",
    )(local_pick, far_weights, local_transfer, *[part[1] for part in parts])
    spread = call(
        functools.partial(spread_body, len(parts), items // leaves, rank),
        shape((256, items), BF16),
        scratch=[
            pltpu.VMEM((256, items), BF16),
            pltpu.VMEM((items, items // leaves), BF16),
            pltpu.VMEM((items, items // leaves), BF16),
        ],
        flops=2e9,
        name="spread",
    )(order, basis_t, far, *[part[0] for part in parts])
    field = call(functools.partial(terms_body, depths[:-1], rank), shape((rank, cols), F32), name="terms")(chains_last, *held)
    product = call(
        functools.partial(final_body, stages - 1, depths[-1], rank, cols), shape((cols, items), BF16), name="final"
    )(gathered, selects, lifts, chains, field, spread)
    return product.T


def solution(mesh):
    return jax.shard_map(
        local,
        mesh=mesh,
        in_specs=(
            P("leaf", None),
            P("leaf", None),
            P("leaf"),
            P("leaf", None),
            P("leaf", None),
            P("leaf", None, None),
            P("leaf", None),
            P(),
            P(),
        ),
        out_specs=P("leaf", None),
        check_vma=False,
    )
```

```python
import functools

import jax
import jax.numpy as jnp
from jax import lax
from jax.experimental import pallas as pl
from jax.experimental.pallas import tpu as pltpu
from jax.sharding import PartitionSpec as P

RIDGE = 1.0
RADICES = {512: (8, 4, 8)}
F32 = jnp.float32
BF16 = jnp.bfloat16
ALL_VMEM = 63 * 1024 * 1024
VMEM_LIMIT = 8 * 1024 * 1024


def dot(a, b):
    return jnp.dot(a, b, preferred_element_type=F32)


def dot_first(a, b):
    return lax.dot_general(a, b, (((0,), (0,)), ((), ())), preferred_element_type=F32)


def dot_last(a, b):
    return lax.dot_general(a, b, (((1,), (1,)), ((), ())), preferred_element_type=F32)


def split(x):
    high = x.astype(BF16)
    return high, (x - high.astype(F32)).astype(BF16)


def dot_wide(a, b):
    a_high, a_low = split(a)
    b_high, b_low = split(b)
    return dot(a_high, b_high) + dot(a_low, b_high) + dot(a_high, b_low)


def dot_right(a, b):
    high, low = split(b)
    return dot(a, high) + dot(a, low)


def dot_first_right(a, b):
    high, low = split(b)
    return dot_first(a, high) + dot_first(a, low)


def dot_first_wide(a, b):
    a_high, a_low = split(a)
    b_high, b_low = split(b)
    return dot_first(a_high, b_high) + dot_first(a_low, b_high) + dot_first(a_high, b_low)


def iota(shape, axis):
    return lax.broadcasted_iota(jnp.int32, shape, axis)


def one_hot(mask):
    return jnp.where(mask, 1.0, 0.0).astype(BF16)


def kernel_of(distance, width):
    return lax.rsqrt(1.0 + jnp.maximum(distance, 0.0) * (1.0 / width))


def self_kernel(points):
    count, width = points.shape
    gram = dot_last(points, points)
    eye = iota(gram.shape, 0) == iota(gram.shape, 1)
    diagonal = jnp.where(eye, gram, 0.0)
    across = jnp.sum(diagonal, axis=1, keepdims=True)
    down = jnp.sum(diagonal, axis=0, keepdims=True)
    return kernel_of(across + down - 2.0 * gram, width), eye


def columns_of(table):
    return table.astype(F32).T.astype(jnp.int32)


def order_column(order_t, leaf):
    return jnp.concatenate([order_t[:, 2 * leaf : 2 * leaf + 1], order_t[:, 2 * leaf + 1 : 2 * leaf + 2]], axis=0)


def order_row(order, leaf):
    return jnp.concatenate([order[2 * leaf : 2 * leaf + 1, :], order[2 * leaf + 1 : 2 * leaf + 2, :]], axis=1)


def padded_columns(tables, rows):
    stacked = jnp.concatenate(tables, axis=0)
    short = rows - stacked.shape[0]
    if short:
        stacked = jnp.concatenate([stacked, jnp.zeros((short, stacked.shape[1]), jnp.int32)], axis=0)
    wide = jnp.concatenate([stacked, jnp.zeros((rows, 128 - stacked.shape[1]), jnp.int32)], axis=1)
    return columns_of(wide)


def fetch(sources, targets, sems):
    copies = [pltpu.make_async_copy(s, t, sems.at[i]) for i, (s, t) in enumerate(zip(sources, targets))]
    for copy in copies:
        copy.start()
    return copies


def digits_of(places, leaf):
    return (places // leaf).astype(F32).astype(BF16), (places & (leaf - 1)).astype(F32).astype(BF16)


def skeleton_ids(leaves, leaf, order, table, rank):
    rows = jnp.concatenate([order[pl.ds(0, leaves, stride=2), :], order[pl.ds(1, leaves, stride=2), :]], axis=1)
    high, low = digits_of(rows, leaf)
    digits = jnp.concatenate([high.astype(F32), low.astype(F32)], axis=0).astype(BF16)
    spots = jnp.concatenate([table[:rank, l : l + 1] for l in range(leaves)], axis=0)
    found = dot_last(one_hot(spots == iota((spots.shape[0], leaf), 1)), digits)
    lane = iota(found.shape, 1)
    own = iota(found.shape, 0) // rank
    block = jnp.sum(jnp.where(lane == own, found, 0.0), axis=1, keepdims=True)
    offset = jnp.sum(jnp.where(lane == own + leaves, found, 0.0), axis=1, keepdims=True)
    lane = iota((spots.shape[0], 128), 1)
    return jnp.where(lane == 0, block, jnp.where(lane == 1, offset, 0.0)).astype(BF16)


def items_of(ids, leaf, emb):
    ids = ids.astype(F32).astype(jnp.int32)
    spots = ids[:, :1] * leaf + ids[:, 1:2]
    return dot(one_hot(spots == iota((ids.shape[0], emb.shape[0]), 1)), emb[...]).astype(BF16)


def picked_of(nodes, parents, table, leaves, rank):
    rows = jnp.concatenate(
        [table[:rank, leaves + q - 1 : leaves + q] + 2 * rank * (q - parents) for q in range(parents, 2 * parents)], axis=0
    )
    return dot(one_hot(rows == iota((parents * rank, nodes.shape[0]), 1)), nodes).astype(BF16)


def pre_body(leaves, *refs):
    sources, (payload, rhs_tree, weights), targets, sems = refs[:7], refs[7:10], refs[10:17], refs[17]
    copies = fetch(sources, targets, sems)
    order, skel, pick, rhs, basis, transfer, emb = targets
    cols, items = rhs.shape
    leaf = items // leaves
    rank = skel.shape[1]
    blocks = items // leaf
    for copy in copies[:6]:
        copy.wait()
    table = padded_columns([skel[...], pick[...]], 16)
    joined = jnp.concatenate([rhs[:, b * leaf : (b + 1) * leaf] for b in range(blocks)], axis=0)

    def gather(l):
        row = jnp.concatenate([order_row(order, l + j) for j in range(4)], axis=1)
        low, high = row & (leaf - 1), row // leaf
        found = dot(joined, one_hot(low == iota((leaf, 4 * leaf), 0)))
        total = None
        for b in range(blocks):
            part = jnp.where(high == b, found[b * cols : (b + 1) * cols, :], 0.0)
            total = part if total is None else total + part
        picked = total.astype(BF16)
        rhs_tree[:, l * leaf : (l + 4) * leaf] = picked
        found = []
        for j in range(4):
            lanes = slice((l + j) * leaf, (l + j + 1) * leaf)
            found.append(dot_last(basis[:, lanes], picked[:, j * leaf : (j + 1) * leaf]))
            weights[(l + j) * rank : (l + j + 1) * rank, :] = found[-1]
        return found

    def lift(q, left, right):
        pair = jnp.concatenate([left, right], axis=0)
        return dot_first_right(transfer[2 * q - 1 : 2 * q + 1].reshape(2 * rank, rank), pair)

    nodes, parents, pending = None, leaves, {}
    for l in range(leaves):
        if l % 4 == 0:
            group = gather(l)
        node, q = group[l % 4], leaves + l
        if l == 1:
            copies[6].wait()
        if l == leaves - 1:
            nodes = items_of(nodes, leaf, emb)
        while q % 2:
            node = lift(q // 2, pending.pop(q - 1), node)
            q //= 2
            if q == 1:
                break
        pending[q] = node
        if nodes is None:
            nodes = skeleton_ids(leaves, leaf, order, table, rank)
        elif parents > 1:
            parents //= 2
            nodes = picked_of(nodes, parents, table, leaves, rank)
    while parents > 1:
        parents //= 2
        nodes = picked_of(nodes, parents, table, leaves, rank)
    own = pending[1]
    share = dot_first_right(transfer[0], own)
    payload[...] = jnp.concatenate([nodes, own.astype(BF16), share.astype(BF16)], axis=1)


def packed(weights, width):
    rank, cols = weights.shape
    rows = rank * cols // width
    return jnp.concatenate([weights[r : r + rows, :] for r in range(0, rank, rows)], axis=1)


def send(payload, points, weights):
    rank, width = points.shape
    points = points.astype(BF16)
    tail = packed(weights, width).astype(BF16)
    for r in range(payload.shape[0]):
        payload[r, :rank, :] = points
        payload[r, rank:, :] = tail


def side_body(rank, me_ref, mine, pick, hot, kept):
    me = me_ref[0]
    devices = pick.shape[1]
    parent = one_hot(iota((8, devices), 1) == (devices + me) // 2)
    spots = dot_last(pick[...].astype(F32).astype(BF16), parent)[:, :1].astype(jnp.int32)
    shift = jnp.where(me % 2 == 0, 0, rank)
    spots = jnp.where(spots >= shift, spots - shift, spots + rank)
    hot[...] = one_hot(spots == iota((rank, 2 * rank), 1))
    kept[...] = mine[...]


def pair_body(rank, cols, hot, mine, other, payload, pairs, siblings):
    width = mine.shape[1] - 2 * cols
    both = jnp.concatenate([mine[:, :width], other[:, :width]], axis=0)
    pairs[...] = both
    siblings[...] = other[:, width : width + cols].astype(F32)
    total = mine[:, width + cols :].astype(F32) + other[:, width + cols :].astype(F32)
    send(payload, dot(hot[...], both), total)


def slots_of(radix):
    starts, at = [], 0
    for h in range(radix.bit_length()):
        starts.append(at)
        at += radix >> h
    return starts


def prep_body(devices, radices, me_ref, pick_hbm, upper_hbm, local_hbm, *refs):
    selects, lifts, chains, select_all, lift_all, pick, upper, own_transfer, rows_of, sems = refs
    copies = fetch((pick_hbm, upper_hbm, local_hbm.at[pl.ds(0, 1)]), (pick, upper, own_transfer), sems)
    rank = own_transfer.shape[1]
    me = me_ref[0]
    most = max(radices)
    slots = 2 * most
    nodes = slots * len(radices)
    here = iota((nodes, devices), 0)
    wanted = jnp.full((nodes, devices), -1, jnp.int32)
    base = 1
    for stage, radix in enumerate(radices):
        depth = radix.bit_length() - 1
        top = (devices + me) // (1 << (base + depth))
        for h, start in enumerate(slots_of(radix)):
            first = stage * slots + start
            inside = (here >= first) & (here < first + (radix >> h))
            wanted = jnp.where(inside, here - first + top * (radix >> h), wanted)
        base += depth
    hot = one_hot(wanted == iota((nodes, devices), 1))
    for copy in copies:
        copy.wait()
    table = dot_last(pick[...].astype(F32).astype(BF16), hot).astype(jnp.int32)
    flat = dot_last(hot, upper[...].reshape(rank * rank, devices))
    for a in range(rank):
        rows_of[a * nodes : (a + 1) * nodes, :] = flat[:, a * rank : (a + 1) * rank]

    def moved_of(slot):
        return rows_of[pl.ds(slot, rank, stride=nodes), :]

    base = 1
    chain = own_transfer[0].astype(F32)
    for stage, radix in enumerate(radices):
        depth = radix.bit_length() - 1
        place = (me // (1 << base)) % radix
        wide = radix * rank
        starts = [rank * s for s in slots_of(radix)]
        eye = iota((wide, wide), 0) == iota((wide, wide), 1)
        select_all[0:wide, :wide] = jnp.where(eye, 1.0, 0.0)
        lift_all[0:wide, :wide] = jnp.where(eye, 1.0, 0.0)
        for h in range(1, depth + 1):
            below, at = starts[h - 1], starts[h]
            for p in range(radix >> h):
                pair = slice(below + 2 * rank * p, below + 2 * rank * (p + 1))
                spot = slice(at + rank * p, at + rank * (p + 1))
                slot = stage * slots + at // rank + p
                picked = one_hot(table[:, slot : slot + 1] == iota((rank, 2 * rank), 1))
                select_all[spot, :wide] = dot(picked, select_all[pair, :wide].astype(BF16))
                child = stage * slots + below // rank + 2 * p
                moved = jnp.concatenate([moved_of(child), moved_of(child + 1)], axis=0).astype(BF16)
                lift_all[spot, :wide] = dot_first_right(moved, lift_all[pair, :wide])
        steps = [place // (1 << h) for h in range(depth)]
        mine = [pl.multiple_of(starts[h] + rank * s, rank) for h, s in enumerate(steps)]
        others = [pl.multiple_of(starts[h] + rank * (s + 1 - 2 * (s % 2)), rank) for h, s in enumerate(steps)]
        for i, spot in enumerate(mine + others + [starts[depth]]):
            selects[stage, i * rank : (i + 1) * rank, :wide] = select_all[pl.ds(spot, rank), :wide].astype(BF16)
        for i, spot in enumerate(others + [starts[depth]]):
            high, low = split(lift_all[pl.ds(spot, rank), :wide])
            lifts[stage, 0, i * rank : (i + 1) * rank, :wide] = high
            lifts[stage, 1, i * rank : (i + 1) * rank, :wide] = low
        for h in range(depth):
            step = moved_of(stage * slots + starts[h] // rank + steps[h]).astype(BF16)
            chains[stage, h * rank : (h + 1) * rank, :] = chain
            high, low = split(chain)
            chain = dot(high, step) + dot(low, step)
        base += depth


def gathered_nodes(rank, cols, gathered, select, lift):
    count, rows, width = gathered.shape
    wide = count * rank
    points = dot(select[:, :wide], gathered[:, :rank, :].reshape(wide, width)).astype(BF16)
    tails = gathered[:, rank:, :].astype(F32)
    parts = [tails[j, :, c : c + cols] for j in range(count) for c in range(0, width, cols)]
    weights = jnp.concatenate(parts, axis=0).astype(BF16)
    return points, dot(lift[0, :, :wide], weights) + dot(lift[1, :, :wide], weights)


def terms_of(own, other, weights, rank):
    count, width = own.shape
    gram = dot_last(own, other)
    own_wide, other_wide = own.astype(F32), other.astype(F32)
    across = jnp.sum(own_wide * own_wide, axis=1, keepdims=True)
    down = jnp.sum(other_wide * other_wide, axis=1, keepdims=True)
    down = jnp.broadcast_to(down, (count, 128)).T[0:1, :]
    kernel = kernel_of(across + down - 2.0 * gram, width)
    same = iota(gram.shape, 0) // rank == iota(gram.shape, 1) // rank
    return dot_wide(jnp.where(same, kernel, 0.0), weights)


def chained(chain, terms, rank):
    total = None
    for h in range(terms.shape[0] // rank):
        part = dot_wide(chain[h * rank : (h + 1) * rank, :], terms[h * rank : (h + 1) * rank, :])
        total = part if total is None else total + part
    return total


def hop_body(stage, depth, rank, cols, gathered, selects, lifts, payload, pairs, siblings):
    rows = depth * rank
    points, lifted = gathered_nodes(
        rank, cols, gathered, selects[stage, : (2 * depth + 1) * rank, :], lifts[stage, :, : rows + rank, :]
    )
    pairs[...] = points[: 2 * rows, :]
    siblings[...] = lifted[:rows, :]
    send(payload, points[2 * rows :, :], lifted[rows:, :])


def terms_body(depths, rank, chains, *refs):
    total = terms_of(refs[0][:rank, :], refs[0][rank:, :], refs[1][...], rank)
    for stage, depth in enumerate(depths):
        pairs, siblings = refs[2 * stage + 2], refs[2 * stage + 3]
        rows = depth * rank
        terms = terms_of(pairs[:rows, :], pairs[rows:, :], siblings[...], rank)
        total = total + chained(chains[stage], terms, rank)
    refs[-1][...] = total


def final_body(stage, depth, rank, cols, gathered, selects, lifts, chains, before, spread, product):
    rows = depth * rank
    points, lifted = gathered_nodes(
        rank, cols, gathered, selects[stage, : 2 * rows, :], lifts[stage, :, :rows, :]
    )
    terms = terms_of(points[:rows, :], points[rows:, :], lifted, rank)
    field = chained(chains[stage], terms, rank) + before[...]
    high = field.astype(BF16).astype(F32)
    low = field - high
    eye = jnp.where(iota((cols, cols), 0) == iota((cols, cols), 1), 1.0, 0.0)
    right = jnp.concatenate([eye, eye, high, high, low, jnp.zeros_like(low)], axis=0).astype(BF16)
    product[...] = dot_first(right, spread[...]).astype(BF16)


def far_body(leaves, parts, rank, cols, pick, weights, transfer, *refs):
    count = leaves
    terms = []
    table = padded_columns([pick[...]], 8)
    points = jnp.concatenate([ref[...] for ref in refs[:parts]], axis=0)
    result = refs[parts]
    level = weights[...]
    while count > 1:
        kernel, _ = self_kernel(points)
        here = iota(kernel.shape, 0) // rank
        there = iota(kernel.shape, 1) // rank
        partner = here + 1 - 2 * (here % 2)
        terms.append(dot_wide(jnp.where(there == partner, kernel, 0.0), level))
        half = count // 2
        if half > 1:
            points = picked_of(points, half, table, 0, rank)
            level = jnp.concatenate(
                [
                    dot_first_right(
                        transfer[2 * q - 1 : 2 * q + 1].reshape(2 * rank, rank),
                        level[2 * rank * (q - half) : 2 * rank * (q - half + 1), :],
                    )
                    for q in range(half, 2 * half)
                ],
                axis=0,
            )
        count = half
    below = None
    for height in reversed(range(len(terms))):
        count = leaves >> height
        nodes = []
        for n in range(count):
            moved = transfer[count + n - 1]
            term = terms[height][n * rank : (n + 1) * rank, :]
            if below is None:
                node = jnp.concatenate([term, moved.astype(F32), jnp.zeros((rank, 128 - cols - rank), F32)], axis=1)
            else:
                pad = jnp.zeros((rank, 128 - cols), F32)
                node = dot_right(moved, below[n // 2]) + jnp.concatenate([term, pad], axis=1)
            nodes.append(node)
        below = nodes
    result[...] = jnp.concatenate(below, axis=0)


def leaf_body(first, count, rank, order, emb, rhs_tree, skel, near, points):
    items = emb.shape[0]
    leaf = near.shape[1] // count
    table = padded_columns([skel[...]], 8)
    turned = emb[...].T
    for i in range(0, count, 4):
        row = jnp.concatenate([order_row(order, first + j) for j in range(i, i + 4)], axis=1)
        offset = one_hot(iota((leaf, 4 * leaf), 0) == (row & (leaf - 1)))
        block = jnp.broadcast_to(digits_of(row, leaf)[0], (leaf, 4 * leaf))
        hot = jnp.concatenate([jnp.where(block == b, offset, jnp.zeros_like(offset)) for b in range(items // leaf)], axis=0)
        both = dot(turned, hot).astype(BF16)
        for j in range(i, i + 4):
            l = first + j
            feats = both[:, (j - i) * leaf : (j - i + 1) * leaf].astype(F32).T.astype(BF16)
            kernel, eye = self_kernel(feats)
            kernel = jnp.where(eye, kernel + RIDGE, kernel).astype(BF16)
            near[:, j * leaf : (j + 1) * leaf] = dot(rhs_tree[:, l * leaf : (l + 1) * leaf], kernel)
            spots = one_hot(table[:rank, l : l + 1] == iota((rank, leaf), 1))
            points[j * rank : (j + 1) * rank, :] = dot(spots, feats).astype(BF16)


def spread_body(parts, leaf, rank, order, basis, far, *refs):
    near, result, tree, offset, block = refs[:parts], refs[parts], refs[parts + 1], refs[parts + 2], refs[parts + 3]
    items = basis.shape[1]
    cols = near[0].shape[0]
    order_t = columns_of(order[...])
    for c in range(order.shape[0]):
        column = order_t[:, c : c + 1]
        rows = slice(c * 128, (c + 1) * 128)
        offset[rows, :] = one_hot(iota((128, leaf), 1) == (column & (leaf - 1)))
        block[rows, :] = jnp.broadcast_to(digits_of(column, leaf)[0], (128, leaf))
    l = 0
    for part in near:
        for i in range(part.shape[1] // leaf):
            lanes = slice(l * leaf, (l + 1) * leaf)
            high, low = split(far[l * rank : (l + 1) * rank, :])
            both = dot_first(high, basis[:, lanes]) + dot_first(low, basis[:, lanes])
            total = part[:, i * leaf : (i + 1) * leaf] + both[:cols, :]
            total_high = total.astype(BF16).astype(F32)
            moved = both[cols : cols + rank, :]
            moved_high = moved.astype(BF16).astype(F32)
            tree[:, lanes] = jnp.concatenate(
                [total_high, total - total_high, moved_high, moved - moved_high, moved_high, jnp.zeros_like(moved)], axis=0
            ).astype(BF16)
            l += 1
    for b in range(items // leaf):
        hot = jnp.where(block[...] == b, offset[...], jnp.zeros_like(offset))
        result[:, b * leaf : (b + 1) * leaf] = dot(tree[...], hot).astype(BF16)


def call(body, outs, scratch=(), flops=1e8, name=None, specs=None, limit=VMEM_LIMIT):
    extra = {} if specs is None else {"in_specs": specs}
    return pl.pallas_call(
        body,
        out_shape=outs,
        scratch_shapes=list(scratch),
        cost_estimate=pl.CostEstimate(flops=int(flops), bytes_accessed=1 << 20, transcendentals=0),
        compiler_params=pltpu.CompilerParams(vmem_limit_bytes=limit),
        name=name,
        **extra,
    )


def after(values, earlier):
    return lax.optimization_barrier((*values, earlier))[:-1]


def shape(dims, dtype):
    return jax.ShapeDtypeStruct(dims, dtype)


def local(
    embeddings,
    rhs,
    item_order,
    leaf_basis,
    leaf_skel,
    local_transfer,
    local_pick,
    upper_transfer,
    upper_pick,
):
    leaves, rank = leaf_skel.shape
    items, cols = rhs.shape
    width = embeddings.shape[1]
    devices = lax.axis_size("leaf")
    radices = RADICES[devices]
    me = lax.axis_index("leaf")
    me = me.astype(jnp.int32).reshape(1)
    order = item_order.reshape(items // 128, 128)
    basis_t = leaf_basis.T
    far_away = pl.BlockSpec(memory_space=pltpu.HBM)

    given = (order, leaf_skel, local_pick, rhs.T, basis_t, local_transfer, embeddings)
    payload, rhs_tree, weights = call(
        functools.partial(pre_body, leaves),
        (
            shape((rank, width + 2 * cols), BF16),
            shape((cols, items), BF16),
            shape((leaves * rank, cols), F32),
        ),
        scratch=[pltpu.VMEM(x.shape, x.dtype) for x in given] + [pltpu.SemaphoreType.DMA((len(given),))],
        specs=[far_away] * len(given),
        limit=ALL_VMEM,
        name="pre",
    )(*given)
    other = lax.ppermute(payload, "leaf", [(i, i ^ 1) for i in range(devices)])
    memory = pl.BlockSpec(memory_space=pltpu.SMEM)
    whole = pl.BlockSpec(memory_space=pltpu.VMEM)
    hot, kept = call(
        functools.partial(side_body, rank),
        (shape((rank, 2 * rank), BF16), shape(payload.shape, BF16)),
        specs=[memory] + [whole] * 2,
        name="side",
    )(me, payload, upper_pick.T)
    sent = rank + rank * cols // width
    payload, pairs, siblings = call(
        functools.partial(pair_body, rank, cols),
        (
            shape((radices[0], sent, width), BF16),
            shape((2 * rank, width), BF16),
            shape((rank, cols), F32),
        ),
        name="pair",
    )(hot, kept, other)
    held = [pairs, siblings]

    stages = len(radices)
    most = max(radices)
    depths = [n.bit_length() - 1 for n in radices]
    deepest = max(depths)
    nodes = 2 * most * stages
    (me,) = after((me,), payload)
    selects, lifts, chains = call(
        functools.partial(prep_body, devices, radices),
        (
            shape((stages, (2 * deepest + 1) * rank, most * rank), BF16),
            shape((stages, 2, (deepest + 1) * rank, most * rank), BF16),
            shape((stages, deepest * rank, rank), F32),
        ),
        scratch=[
            pltpu.VMEM((2 * most * rank, most * rank), F32),
            pltpu.VMEM((2 * most * rank, most * rank), F32),
            pltpu.VMEM((rank, devices), jnp.int32),
            pltpu.VMEM((rank, rank, devices), BF16),
            pltpu.VMEM((1, rank, rank), BF16),
            pltpu.VMEM((rank * nodes, rank), F32),
            pltpu.SemaphoreType.DMA((3,)),
        ],
        specs=[memory] + [far_away] * 3,
        flops=2e9,
        name="prep",
    )(me, upper_pick.T, upper_transfer.transpose(1, 2, 0), local_transfer)

    def leaf_part(first, count, earlier):
        return call(
            functools.partial(leaf_body, first, count, rank),
            (shape((cols, items // leaves * count), F32), shape((count * rank, width), BF16)),
            flops=2e9,
            name="leaf",
        )(after((order,), earlier)[0], embeddings, rhs_tree, leaf_skel)

    lead = leaves // 2
    parts = [leaf_part(0, lead, chains)]
    base = 1
    for stage, (n, depth) in enumerate(zip(radices, depths)):
        stride = 1 << base
        groups = [
            [high * stride * n + low + stride * j for j in range(n)]
            for high in range(devices // (stride * n))
            for low in range(stride)
        ]
        gathered = lax.all_to_all(payload, "leaf", 0, 0, axis_index_groups=groups)
        base += depth
        if stage == 1:
            parts.append(leaf_part(lead, leaves - lead, payload))
        if stage + 1 < stages:
            gathered, *held_points = lax.optimization_barrier((gathered, *parts[-1]))
            parts[-1] = held_points
        if stage + 1 < stages:
            payload, pairs, siblings = call(
                functools.partial(hop_body, stage, depth, rank, cols),
                (
                    shape((radices[stage + 1], sent, width), BF16),
                    shape((2 * depth * rank, width), BF16),
                    shape((depth * rank, cols), F32),
                ),
                name="hop",
            )(gathered, selects, lifts)
            held += [pairs, siblings]
    chains_last, far_weights = after((chains, weights), payload)
    far = call(
        functools.partial(far_body, leaves, len(parts), rank, cols),
        shape((leaves * rank, 128), F32),
        flops=1e9,
        name="far",
    )(local_pick, far_weights, local_transfer, *[part[1] for part in parts])
    spread = call(
        functools.partial(spread_body, len(parts), items // leaves, rank),
        shape((256, items), BF16),
        scratch=[
            pltpu.VMEM((256, items), BF16),
            pltpu.VMEM((items, items // leaves), BF16),
            pltpu.VMEM((items, items // leaves), BF16),
        ],
        flops=2e9,
        name="spread",
    )(order, basis_t, far, *[part[0] for part in parts])
    field = call(functools.partial(terms_body, depths[:-1], rank), shape((rank, cols), F32), name="terms")(chains_last, *held)
    product = call(
        functools.partial(final_body, stages - 1, depths[-1], rank, cols), shape((cols, items), BF16), name="final"
    )(gathered, selects, lifts, chains, field, spread)
    return product.T


def solution(mesh):
    return jax.shard_map(
        local,
        mesh=mesh,
        in_specs=(
            P("leaf", None),
            P("leaf", None),
            P("leaf"),
            P("leaf", None),
            P("leaf", None),
            P("leaf", None, None),
            P("leaf", None),
            P(),
            P(),
        ),
        out_specs=P("leaf", None),
        check_vma=False,
    )
```

```python
import functools

import jax
import jax.numpy as jnp
from jax import lax
from jax.experimental import pallas as pl
from jax.experimental.pallas import tpu as pltpu
from jax.sharding import PartitionSpec as P

RIDGE = 1.0
RADICES = {512: (8, 4, 8)}
F32 = jnp.float32
BF16 = jnp.bfloat16
ALL_VMEM = 63 * 1024 * 1024
VMEM_LIMIT = 8 * 1024 * 1024


def dot(a, b):
    return jnp.dot(a, b, preferred_element_type=F32)


def dot_first(a, b):
    return lax.dot_general(a, b, (((0,), (0,)), ((), ())), preferred_element_type=F32)


def dot_last(a, b):
    return lax.dot_general(a, b, (((1,), (1,)), ((), ())), preferred_element_type=F32)


def split(x):
    high = x.astype(BF16)
    return high, (x - high.astype(F32)).astype(BF16)


def dot_wide(a, b):
    a_high, a_low = split(a)
    b_high, b_low = split(b)
    return dot(a_high, b_high) + dot(a_low, b_high) + dot(a_high, b_low)


def dot_right(a, b):
    high, low = split(b)
    return dot(a, high) + dot(a, low)


def dot_first_right(a, b):
    high, low = split(b)
    return dot_first(a, high) + dot_first(a, low)


def dot_first_wide(a, b):
    a_high, a_low = split(a)
    b_high, b_low = split(b)
    return dot_first(a_high, b_high) + dot_first(a_low, b_high) + dot_first(a_high, b_low)


def iota(shape, axis):
    return lax.broadcasted_iota(jnp.int32, shape, axis)


def one_hot(mask):
    return jnp.where(mask, 1.0, 0.0).astype(BF16)


def kernel_of(distance, width):
    return lax.rsqrt(1.0 + jnp.maximum(distance, 0.0) * (1.0 / width))


def self_kernel(points):
    count, width = points.shape
    gram = dot_last(points, points)
    eye = iota(gram.shape, 0) == iota(gram.shape, 1)
    diagonal = jnp.where(eye, gram, 0.0)
    across = jnp.sum(diagonal, axis=1, keepdims=True)
    down = jnp.sum(diagonal, axis=0, keepdims=True)
    return kernel_of(across + down - 2.0 * gram, width), eye


def columns_of(table):
    return table.astype(F32).T.astype(jnp.int32)


def order_column(order_t, leaf):
    return jnp.concatenate([order_t[:, 2 * leaf : 2 * leaf + 1], order_t[:, 2 * leaf + 1 : 2 * leaf + 2]], axis=0)


def order_row(order, leaf):
    return jnp.concatenate([order[2 * leaf : 2 * leaf + 1, :], order[2 * leaf + 1 : 2 * leaf + 2, :]], axis=1)


def padded_columns(tables, rows):
    stacked = jnp.concatenate(tables, axis=0)
    short = rows - stacked.shape[0]
    if short:
        stacked = jnp.concatenate([stacked, jnp.zeros((short, stacked.shape[1]), jnp.int32)], axis=0)
    wide = jnp.concatenate([stacked, jnp.zeros((rows, 128 - stacked.shape[1]), jnp.int32)], axis=1)
    return columns_of(wide)


def fetch(sources, targets, sems):
    copies = [pltpu.make_async_copy(s, t, sems.at[i]) for i, (s, t) in enumerate(zip(sources, targets))]
    for copy in copies:
        copy.start()
    return copies


def digits_of(places, leaf):
    return (places // leaf).astype(F32).astype(BF16), (places & (leaf - 1)).astype(F32).astype(BF16)


def skeleton_ids(leaves, leaf, order, table, rank):
    rows = jnp.concatenate([order[pl.ds(0, leaves, stride=2), :], order[pl.ds(1, leaves, stride=2), :]], axis=1)
    high, low = digits_of(rows, leaf)
    digits = jnp.concatenate([high.astype(F32), low.astype(F32)], axis=0).astype(BF16)
    spots = jnp.concatenate([table[:rank, l : l + 1] for l in range(leaves)], axis=0)
    found = dot_last(one_hot(spots == iota((spots.shape[0], leaf), 1)), digits)
    lane = iota(found.shape, 1)
    own = iota(found.shape, 0) // rank
    block = jnp.sum(jnp.where(lane == own, found, 0.0), axis=1, keepdims=True)
    offset = jnp.sum(jnp.where(lane == own + leaves, found, 0.0), axis=1, keepdims=True)
    lane = iota((spots.shape[0], 128), 1)
    return jnp.where(lane == 0, block, jnp.where(lane == 1, offset, 0.0)).astype(BF16)


def items_of(ids, leaf, emb):
    ids = ids.astype(F32).astype(jnp.int32)
    spots = ids[:, :1] * leaf + ids[:, 1:2]
    return dot(one_hot(spots == iota((ids.shape[0], emb.shape[0]), 1)), emb[...]).astype(BF16)


def picked_of(nodes, parents, table, leaves, rank):
    rows = jnp.concatenate(
        [table[:rank, leaves + q - 1 : leaves + q] + 2 * rank * (q - parents) for q in range(parents, 2 * parents)], axis=0
    )
    return dot(one_hot(rows == iota((parents * rank, nodes.shape[0]), 1)), nodes).astype(BF16)


def pre_body(leaves, *refs):
    sources, (payload, rhs_tree, weights), targets, sems = refs[:7], refs[7:10], refs[10:17], refs[17]
    copies = fetch(sources, targets, sems)
    order, skel, pick, rhs, basis, transfer, emb = targets
    cols, items = rhs.shape
    leaf = items // leaves
    rank = skel.shape[1]
    blocks = items // leaf
    for copy in copies[:6]:
        copy.wait()
    table = padded_columns([skel[...], pick[...]], 16)
    joined = jnp.concatenate([rhs[:, b * leaf : (b + 1) * leaf] for b in range(blocks)], axis=0)

    def gather(l):
        row = jnp.concatenate([order_row(order, l + j) for j in range(4)], axis=1)
        low, high = row & (leaf - 1), row // leaf
        found = dot(joined, one_hot(low == iota((leaf, 4 * leaf), 0)))
        total = None
        for b in range(blocks):
            part = jnp.where(high == b, found[b * cols : (b + 1) * cols, :], 0.0)
            total = part if total is None else total + part
        picked = total.astype(BF16)
        rhs_tree[:, l * leaf : (l + 4) * leaf] = picked
        found = []
        for j in range(4):
            lanes = slice((l + j) * leaf, (l + j + 1) * leaf)
            found.append(dot_last(basis[:, lanes], picked[:, j * leaf : (j + 1) * leaf]))
            weights[(l + j) * rank : (l + j + 1) * rank, :] = found[-1]
        return found

    def lift(q, left, right):
        pair = jnp.concatenate([left, right], axis=0)
        return dot_first_right(transfer[2 * q - 1 : 2 * q + 1].reshape(2 * rank, rank), pair)

    nodes, parents, pending = None, leaves, {}
    for l in range(leaves):
        if l % 4 == 0:
            group = gather(l)
        node, q = group[l % 4], leaves + l
        if l == 1:
            copies[6].wait()
        if l == leaves - 1:
            nodes = items_of(nodes, leaf, emb)
        while q % 2:
            node = lift(q // 2, pending.pop(q - 1), node)
            q //= 2
            if q == 1:
                break
        pending[q] = node
        if nodes is None:
            nodes = skeleton_ids(leaves, leaf, order, table, rank)
        elif parents > 1:
            parents //= 2
            nodes = picked_of(nodes, parents, table, leaves, rank)
    while parents > 1:
        parents //= 2
        nodes = picked_of(nodes, parents, table, leaves, rank)
    own = pending[1]
    share = dot_first_right(transfer[0], own)
    payload[...] = jnp.concatenate([nodes, own.astype(BF16), share.astype(BF16)], axis=1)


def packed(weights, width):
    rank, cols = weights.shape
    rows = rank * cols // width
    return jnp.concatenate([weights[r : r + rows, :] for r in range(0, rank, rows)], axis=1)


def send(payload, points, weights):
    rank, width = points.shape
    points = points.astype(BF16)
    tail = packed(weights, width).astype(BF16)
    for r in range(payload.shape[0]):
        payload[r, :rank, :] = points
        payload[r, rank:, :] = tail


def side_body(rank, me_ref, mine, pick, hot, kept):
    me = me_ref[0]
    devices = pick.shape[1]
    parent = one_hot(iota((8, devices), 1) == (devices + me) // 2)
    spots = dot_last(pick[...].astype(F32).astype(BF16), parent)[:, :1].astype(jnp.int32)
    shift = jnp.where(me % 2 == 0, 0, rank)
    spots = jnp.where(spots >= shift, spots - shift, spots + rank)
    hot[...] = one_hot(spots == iota((rank, 2 * rank), 1))
    kept[...] = mine[...]


def pair_body(rank, cols, hot, mine, other, payload, pairs, siblings):
    width = mine.shape[1] - 2 * cols
    both = jnp.concatenate([mine[:, :width], other[:, :width]], axis=0)
    pairs[...] = both
    siblings[...] = other[:, width : width + cols].astype(F32)
    total = mine[:, width + cols :].astype(F32) + other[:, width + cols :].astype(F32)
    send(payload, dot(hot[...], both), total)


def slots_of(radix):
    starts, at = [], 0
    for h in range(radix.bit_length()):
        starts.append(at)
        at += radix >> h
    return starts


def prep_body(devices, radices, me_ref, pick_hbm, upper_hbm, local_hbm, *refs):
    selects, lifts, chains, select_all, lift_all, pick, upper, own_transfer, rows_of, sems = refs
    copies = fetch((pick_hbm, upper_hbm, local_hbm.at[pl.ds(0, 1)]), (pick, upper, own_transfer), sems)
    rank = own_transfer.shape[1]
    me = me_ref[0]
    most = max(radices)
    slots = 2 * most
    nodes = slots * len(radices)
    here = iota((nodes, devices), 0)
    wanted = jnp.full((nodes, devices), -1, jnp.int32)
    base = 1
    for stage, radix in enumerate(radices):
        depth = radix.bit_length() - 1
        top = (devices + me) // (1 << (base + depth))
        for h, start in enumerate(slots_of(radix)):
            first = stage * slots + start
            inside = (here >= first) & (here < first + (radix >> h))
            wanted = jnp.where(inside, here - first + top * (radix >> h), wanted)
        base += depth
    hot = one_hot(wanted == iota((nodes, devices), 1))
    for copy in copies:
        copy.wait()
    table = dot_last(pick[...].astype(F32).astype(BF16), hot).astype(jnp.int32)
    flat = dot_last(hot, upper[...].reshape(rank * rank, devices))
    for a in range(rank):
        rows_of[a * nodes : (a + 1) * nodes, :] = flat[:, a * rank : (a + 1) * rank]

    def moved_of(slot):
        return rows_of[pl.ds(slot, rank, stride=nodes), :]

    base = 1
    chain = own_transfer[0].astype(F32)
    for stage, radix in enumerate(radices):
        depth = radix.bit_length() - 1
        place = (me // (1 << base)) % radix
        wide = radix * rank
        starts = [rank * s for s in slots_of(radix)]
        eye = iota((wide, wide), 0) == iota((wide, wide), 1)
        select_all[0:wide, :wide] = jnp.where(eye, 1.0, 0.0)
        lift_all[0:wide, :wide] = jnp.where(eye, 1.0, 0.0)
        for h in range(1, depth + 1):
            below, at = starts[h - 1], starts[h]
            for p in range(radix >> h):
                pair = slice(below + 2 * rank * p, below + 2 * rank * (p + 1))
                spot = slice(at + rank * p, at + rank * (p + 1))
                slot = stage * slots + at // rank + p
                picked = one_hot(table[:, slot : slot + 1] == iota((rank, 2 * rank), 1))
                select_all[spot, :wide] = dot(picked, select_all[pair, :wide].astype(BF16))
                child = stage * slots + below // rank + 2 * p
                moved = jnp.concatenate([moved_of(child), moved_of(child + 1)], axis=0).astype(BF16)
                lift_all[spot, :wide] = dot_first_right(moved, lift_all[pair, :wide])
        steps = [place // (1 << h) for h in range(depth)]
        mine = [pl.multiple_of(starts[h] + rank * s, rank) for h, s in enumerate(steps)]
        others = [pl.multiple_of(starts[h] + rank * (s + 1 - 2 * (s % 2)), rank) for h, s in enumerate(steps)]
        for i, spot in enumerate(mine + others + [starts[depth]]):
            selects[stage, i * rank : (i + 1) * rank, :wide] = select_all[pl.ds(spot, rank), :wide].astype(BF16)
        for i, spot in enumerate(others + [starts[depth]]):
            high, low = split(lift_all[pl.ds(spot, rank), :wide])
            lifts[stage, 0, i * rank : (i + 1) * rank, :wide] = high
            lifts[stage, 1, i * rank : (i + 1) * rank, :wide] = low
        for h in range(depth):
            step = moved_of(stage * slots + starts[h] // rank + steps[h]).astype(BF16)
            chains[stage, h * rank : (h + 1) * rank, :] = chain
            high, low = split(chain)
            chain = dot(high, step) + dot(low, step)
        base += depth


def gathered_nodes(rank, cols, gathered, select, lift, turned=False):
    count, rows, width = gathered.shape
    wide = count * rank
    places = range(count)[::-1] if turned else range(count)
    points = dot(select[:, :wide], jnp.concatenate([gathered[j, :rank, :] for j in places], axis=0)).astype(BF16)
    tails = gathered[:, rank:, :].astype(F32)
    parts = [tails[j, :, c : c + cols] for j in places for c in range(0, width, cols)]
    weights = jnp.concatenate(parts, axis=0).astype(BF16)
    return points, dot(lift[0, :, :wide], weights) + dot(lift[1, :, :wide], weights)


def terms_of(own, other, weights, rank):
    count, width = own.shape
    gram = dot_last(own, other)
    own_wide, other_wide = own.astype(F32), other.astype(F32)
    across = jnp.sum(own_wide * own_wide, axis=1, keepdims=True)
    down = jnp.sum(other_wide * other_wide, axis=1, keepdims=True)
    down = jnp.broadcast_to(down, (count, 128)).T[0:1, :]
    kernel = kernel_of(across + down - 2.0 * gram, width)
    same = iota(gram.shape, 0) // rank == iota(gram.shape, 1) // rank
    return dot_wide(jnp.where(same, kernel, 0.0), weights)


def chained(chain, terms, rank):
    total = None
    for h in range(terms.shape[0] // rank):
        part = dot_wide(chain[h * rank : (h + 1) * rank, :], terms[h * rank : (h + 1) * rank, :])
        total = part if total is None else total + part
    return total


def hop_body(stage, depth, rank, cols, gathered, selects, lifts, payload, pairs, siblings):
    rows = depth * rank
    points, lifted = gathered_nodes(
        rank, cols, gathered, selects[stage, : (2 * depth + 1) * rank, :], lifts[stage, :, : rows + rank, :]
    )
    pairs[...] = points[: 2 * rows, :]
    siblings[...] = lifted[:rows, :]
    send(payload, points[2 * rows :, :], lifted[rows:, :])


def terms_body(depths, rank, chains, *refs):
    total = terms_of(refs[0][:rank, :], refs[0][rank:, :], refs[1][...], rank)
    for stage, depth in enumerate(depths):
        pairs, siblings = refs[2 * stage + 2], refs[2 * stage + 3]
        rows = depth * rank
        terms = terms_of(pairs[:rows, :], pairs[rows:, :], siblings[...], rank)
        total = total + chained(chains[stage], terms, rank)
    refs[-1][...] = total


def final_body(stage, depth, rank, cols, gathered, selects, lifts, chains, before, spread, product):
    rows = depth * rank
    points, lifted = gathered_nodes(
        rank, cols, gathered, selects[stage, : 2 * rows, :], lifts[stage, :, :rows, :], turned=True
    )
    terms = terms_of(points[:rows, :], points[rows:, :], lifted, rank)
    field = chained(chains[stage], terms, rank) + before[...]
    high = field.astype(BF16).astype(F32)
    low = field - high
    eye = jnp.where(iota((cols, cols), 0) == iota((cols, cols), 1), 1.0, 0.0)
    right = jnp.concatenate([eye, eye, high, high, low, jnp.zeros_like(low)], axis=0).astype(BF16)
    product[...] = dot_first(right, spread[...]).astype(BF16)


def far_body(leaves, parts, rank, cols, pick, weights, transfer, *refs):
    count = leaves
    terms = []
    table = padded_columns([pick[...]], 8)
    points = jnp.concatenate([ref[...] for ref in refs[:parts]], axis=0)
    result = refs[parts]
    level = weights[...]
    while count > 1:
        kernel, _ = self_kernel(points)
        here = iota(kernel.shape, 0) // rank
        there = iota(kernel.shape, 1) // rank
        partner = here + 1 - 2 * (here % 2)
        terms.append(dot_wide(jnp.where(there == partner, kernel, 0.0), level))
        half = count // 2
        if half > 1:
            points = picked_of(points, half, table, 0, rank)
            level = jnp.concatenate(
                [
                    dot_first_right(
                        transfer[2 * q - 1 : 2 * q + 1].reshape(2 * rank, rank),
                        level[2 * rank * (q - half) : 2 * rank * (q - half + 1), :],
                    )
                    for q in range(half, 2 * half)
                ],
                axis=0,
            )
        count = half
    below = None
    for height in reversed(range(len(terms))):
        count = leaves >> height
        nodes = []
        for n in range(count):
            moved = transfer[count + n - 1]
            term = terms[height][n * rank : (n + 1) * rank, :]
            if below is None:
                node = jnp.concatenate([term, moved.astype(F32), jnp.zeros((rank, 128 - cols - rank), F32)], axis=1)
            else:
                pad = jnp.zeros((rank, 128 - cols), F32)
                node = dot_right(moved, below[n // 2]) + jnp.concatenate([term, pad], axis=1)
            nodes.append(node)
        below = nodes
    result[...] = jnp.concatenate(below, axis=0)


def leaf_body(first, count, rank, order, emb, rhs_tree, skel, near, points):
    items = emb.shape[0]
    leaf = near.shape[1] // count
    table = padded_columns([skel[...]], 8)
    turned = emb[...].T
    for i in range(0, count, 4):
        row = jnp.concatenate([order_row(order, first + j) for j in range(i, i + 4)], axis=1)
        offset = one_hot(iota((leaf, 4 * leaf), 0) == (row & (leaf - 1)))
        block = jnp.broadcast_to(digits_of(row, leaf)[0], (leaf, 4 * leaf))
        hot = jnp.concatenate([jnp.where(block == b, offset, jnp.zeros_like(offset)) for b in range(items // leaf)], axis=0)
        both = dot(turned, hot).astype(BF16)
        for j in range(i, i + 4):
            l = first + j
            feats = both[:, (j - i) * leaf : (j - i + 1) * leaf].astype(F32).T.astype(BF16)
            kernel, eye = self_kernel(feats)
            kernel = jnp.where(eye, kernel + RIDGE, kernel).astype(BF16)
            near[:, j * leaf : (j + 1) * leaf] = dot(rhs_tree[:, l * leaf : (l + 1) * leaf], kernel)
            spots = one_hot(table[:rank, l : l + 1] == iota((rank, leaf), 1))
            points[j * rank : (j + 1) * rank, :] = dot(spots, feats).astype(BF16)


def spread_body(parts, leaf, rank, order, basis, far, *refs):
    near, result, tree, offset, block = refs[:parts], refs[parts], refs[parts + 1], refs[parts + 2], refs[parts + 3]
    items = basis.shape[1]
    cols = near[0].shape[0]
    order_t = columns_of(order[...])
    for c in range(order.shape[0]):
        column = order_t[:, c : c + 1]
        rows = slice(c * 128, (c + 1) * 128)
        offset[rows, :] = one_hot(iota((128, leaf), 1) == (column & (leaf - 1)))
        block[rows, :] = jnp.broadcast_to(digits_of(column, leaf)[0], (128, leaf))
    l = 0
    for part in near:
        for i in range(part.shape[1] // leaf):
            lanes = slice(l * leaf, (l + 1) * leaf)
            high, low = split(far[l * rank : (l + 1) * rank, :])
            both = dot_first(high, basis[:, lanes]) + dot_first(low, basis[:, lanes])
            total = part[:, i * leaf : (i + 1) * leaf] + both[:cols, :]
            total_high = total.astype(BF16).astype(F32)
            moved = both[cols : cols + rank, :]
            moved_high = moved.astype(BF16).astype(F32)
            tree[:, lanes] = jnp.concatenate(
                [total_high, total - total_high, moved_high, moved - moved_high, moved_high, jnp.zeros_like(moved)], axis=0
            ).astype(BF16)
            l += 1
    for b in range(items // leaf):
        hot = jnp.where(block[...] == b, offset[...], jnp.zeros_like(offset))
        result[:, b * leaf : (b + 1) * leaf] = dot(tree[...], hot).astype(BF16)


def call(body, outs, scratch=(), flops=1e8, name=None, specs=None, limit=VMEM_LIMIT):
    extra = {} if specs is None else {"in_specs": specs}
    return pl.pallas_call(
        body,
        out_shape=outs,
        scratch_shapes=list(scratch),
        cost_estimate=pl.CostEstimate(flops=int(flops), bytes_accessed=1 << 20, transcendentals=0),
        compiler_params=pltpu.CompilerParams(vmem_limit_bytes=limit),
        name=name,
        **extra,
    )


def after(values, earlier):
    return lax.optimization_barrier((*values, earlier))[:-1]


def shape(dims, dtype):
    return jax.ShapeDtypeStruct(dims, dtype)


def local(
    embeddings,
    rhs,
    item_order,
    leaf_basis,
    leaf_skel,
    local_transfer,
    local_pick,
    upper_transfer,
    upper_pick,
):
    leaves, rank = leaf_skel.shape
    items, cols = rhs.shape
    width = embeddings.shape[1]
    devices = lax.axis_size("leaf")
    radices = RADICES[devices]
    me = lax.axis_index("leaf")
    me = me.astype(jnp.int32).reshape(1)
    order = item_order.reshape(items // 128, 128)
    basis_t = leaf_basis.T
    far_away = pl.BlockSpec(memory_space=pltpu.HBM)

    given = (order, leaf_skel, local_pick, rhs.T, basis_t, local_transfer, embeddings)
    payload, rhs_tree, weights = call(
        functools.partial(pre_body, leaves),
        (
            shape((rank, width + 2 * cols), BF16),
            shape((cols, items), BF16),
            shape((leaves * rank, cols), F32),
        ),
        scratch=[pltpu.VMEM(x.shape, x.dtype) for x in given] + [pltpu.SemaphoreType.DMA((len(given),))],
        specs=[far_away] * len(given),
        limit=ALL_VMEM,
        name="pre",
    )(*given)
    other = lax.ppermute(payload, "leaf", [(i, i ^ 1) for i in range(devices)])
    memory = pl.BlockSpec(memory_space=pltpu.SMEM)
    whole = pl.BlockSpec(memory_space=pltpu.VMEM)
    hot, kept = call(
        functools.partial(side_body, rank),
        (shape((rank, 2 * rank), BF16), shape(payload.shape, BF16)),
        specs=[memory] + [whole] * 2,
        name="side",
    )(me, payload, upper_pick.T)
    sent = rank + rank * cols // width
    payload, pairs, siblings = call(
        functools.partial(pair_body, rank, cols),
        (
            shape((radices[0], sent, width), BF16),
            shape((2 * rank, width), BF16),
            shape((rank, cols), F32),
        ),
        name="pair",
    )(hot, kept, other)
    held = [pairs, siblings]

    stages = len(radices)
    most = max(radices)
    depths = [n.bit_length() - 1 for n in radices]
    deepest = max(depths)
    nodes = 2 * most * stages
    (me,) = after((me,), payload)
    selects, lifts, chains = call(
        functools.partial(prep_body, devices, radices),
        (
            shape((stages, (2 * deepest + 1) * rank, most * rank), BF16),
            shape((stages, 2, (deepest + 1) * rank, most * rank), BF16),
            shape((stages, deepest * rank, rank), F32),
        ),
        scratch=[
            pltpu.VMEM((2 * most * rank, most * rank), F32),
            pltpu.VMEM((2 * most * rank, most * rank), F32),
            pltpu.VMEM((rank, devices), jnp.int32),
            pltpu.VMEM((rank, rank, devices), BF16),
            pltpu.VMEM((1, rank, rank), BF16),
            pltpu.VMEM((rank * nodes, rank), F32),
            pltpu.SemaphoreType.DMA((3,)),
        ],
        specs=[memory] + [far_away] * 3,
        flops=2e9,
        name="prep",
    )(me, upper_pick.T, upper_transfer.transpose(1, 2, 0), local_transfer)

    def leaf_part(first, count, earlier):
        return call(
            functools.partial(leaf_body, first, count, rank),
            (shape((cols, items // leaves * count), F32), shape((count * rank, width), BF16)),
            flops=2e9,
            name="leaf",
        )(after((order,), earlier)[0], embeddings, rhs_tree, leaf_skel)

    lead = leaves // 2
    parts = [leaf_part(0, lead, chains)]
    base = 1
    for stage, (n, depth) in enumerate(zip(radices, depths)):
        stride = 1 << base
        groups = [
            [high * stride * n + low + stride * j for j in (range(n) if stage + 1 < stages else range(n)[::-1])]
            for high in range(devices // (stride * n))
            for low in range(stride)
        ]
        gathered = lax.all_to_all(payload, "leaf", 0, 0, axis_index_groups=groups)
        base += depth
        if stage == 1:
            parts.append(leaf_part(lead, leaves - lead, payload))
        if stage + 1 < stages:
            gathered, *held_points = lax.optimization_barrier((gathered, *parts[-1]))
            parts[-1] = held_points
        if stage + 1 < stages:
            payload, pairs, siblings = call(
                functools.partial(hop_body, stage, depth, rank, cols),
                (
                    shape((radices[stage + 1], sent, width), BF16),
                    shape((2 * depth * rank, width), BF16),
                    shape((depth * rank, cols), F32),
                ),
                name="hop",
            )(gathered, selects, lifts)
            held += [pairs, siblings]
    chains_last, far_weights = after((chains, weights), payload)
    far = call(
        functools.partial(far_body, leaves, len(parts), rank, cols),
        shape((leaves * rank, 128), F32),
        flops=1e9,
        name="far",
    )(local_pick, far_weights, local_transfer, *[part[1] for part in parts])
    spread = call(
        functools.partial(spread_body, len(parts), items // leaves, rank),
        shape((256, items), BF16),
        scratch=[
            pltpu.VMEM((256, items), BF16),
            pltpu.VMEM((items, items // leaves), BF16),
            pltpu.VMEM((items, items // leaves), BF16),
        ],
        flops=2e9,
        name="spread",
    )(order, basis_t, far, *[part[0] for part in parts])
    field = call(functools.partial(terms_body, depths[:-1], rank), shape((rank, cols), F32), name="terms")(chains_last, *held)
    product = call(
        functools.partial(final_body, stages - 1, depths[-1], rank, cols), shape((cols, items), BF16), name="final"
    )(gathered, selects, lifts, chains, field, spread)
    return product.T


def solution(mesh):
    return jax.shard_map(
        local,
        mesh=mesh,
        in_specs=(
            P("leaf", None),
            P("leaf", None),
            P("leaf"),
            P("leaf", None),
            P("leaf", None),
            P("leaf", None, None),
            P("leaf", None),
            P(),
            P(),
        ),
        out_specs=P("leaf", None),
        check_vma=False,
    )
```

```python
import functools

import jax
import jax.numpy as jnp
from jax import lax
from jax.experimental import pallas as pl
from jax.experimental.pallas import tpu as pltpu
from jax.sharding import PartitionSpec as P

RIDGE = 1.0
RADICES = {512: (8, 4, 8)}
F32 = jnp.float32
BF16 = jnp.bfloat16
ALL_VMEM = 63 * 1024 * 1024
VMEM_LIMIT = 8 * 1024 * 1024


def dot(a, b):
    return jnp.dot(a, b, preferred_element_type=F32)


def dot_first(a, b):
    return lax.dot_general(a, b, (((0,), (0,)), ((), ())), preferred_element_type=F32)


def dot_last(a, b):
    return lax.dot_general(a, b, (((1,), (1,)), ((), ())), preferred_element_type=F32)


def split(x):
    high = x.astype(BF16)
    return high, (x - high.astype(F32)).astype(BF16)


def dot_wide(a, b):
    a_high, a_low = split(a)
    b_high, b_low = split(b)
    return dot(a_high, b_high) + dot(a_low, b_high) + dot(a_high, b_low)


def dot_right(a, b):
    high, low = split(b)
    return dot(a, high) + dot(a, low)


def dot_first_right(a, b):
    high, low = split(b)
    return dot_first(a, high) + dot_first(a, low)


def dot_first_wide(a, b):
    a_high, a_low = split(a)
    b_high, b_low = split(b)
    return dot_first(a_high, b_high) + dot_first(a_low, b_high) + dot_first(a_high, b_low)


def iota(shape, axis):
    return lax.broadcasted_iota(jnp.int32, shape, axis)


def one_hot(mask):
    return jnp.where(mask, 1.0, 0.0).astype(BF16)


def kernel_of(distance, width):
    return lax.rsqrt(1.0 + jnp.maximum(distance, 0.0) * (1.0 / width))


def self_kernel(points):
    count, width = points.shape
    gram = dot_last(points, points)
    eye = iota(gram.shape, 0) == iota(gram.shape, 1)
    diagonal = jnp.where(eye, gram, 0.0)
    across = jnp.sum(diagonal, axis=1, keepdims=True)
    down = jnp.sum(diagonal, axis=0, keepdims=True)
    return kernel_of(across + down - 2.0 * gram, width), eye


def columns_of(table):
    return table.astype(F32).T.astype(jnp.int32)


def order_column(order_t, leaf):
    return jnp.concatenate([order_t[:, 2 * leaf : 2 * leaf + 1], order_t[:, 2 * leaf + 1 : 2 * leaf + 2]], axis=0)


def order_row(order, leaf):
    return jnp.concatenate([order[2 * leaf : 2 * leaf + 1, :], order[2 * leaf + 1 : 2 * leaf + 2, :]], axis=1)


def padded_columns(tables, rows):
    stacked = jnp.concatenate(tables, axis=0)
    short = rows - stacked.shape[0]
    if short:
        stacked = jnp.concatenate([stacked, jnp.zeros((short, stacked.shape[1]), jnp.int32)], axis=0)
    wide = jnp.concatenate([stacked, jnp.zeros((rows, 128 - stacked.shape[1]), jnp.int32)], axis=1)
    return columns_of(wide)


def fetch(sources, targets, sems):
    copies = [pltpu.make_async_copy(s, t, sems.at[i]) for i, (s, t) in enumerate(zip(sources, targets))]
    for copy in copies:
        copy.start()
    return copies


def digits_of(places, leaf):
    return (places // leaf).astype(F32).astype(BF16), (places & (leaf - 1)).astype(F32).astype(BF16)


def skeleton_ids(leaves, leaf, order, table, rank):
    rows = jnp.concatenate([order[pl.ds(0, leaves, stride=2), :], order[pl.ds(1, leaves, stride=2), :]], axis=1)
    high, low = digits_of(rows, leaf)
    digits = jnp.concatenate([high.astype(F32), low.astype(F32)], axis=0).astype(BF16)
    spots = jnp.concatenate([table[:rank, l : l + 1] for l in range(leaves)], axis=0)
    found = dot_last(one_hot(spots == iota((spots.shape[0], leaf), 1)), digits)
    lane = iota(found.shape, 1)
    own = iota(found.shape, 0) // rank
    block = jnp.sum(jnp.where(lane == own, found, 0.0), axis=1, keepdims=True)
    offset = jnp.sum(jnp.where(lane == own + leaves, found, 0.0), axis=1, keepdims=True)
    lane = iota((spots.shape[0], 128), 1)
    return jnp.where(lane == 0, block, jnp.where(lane == 1, offset, 0.0)).astype(BF16)


def items_of(ids, leaf, emb):
    ids = ids.astype(F32).astype(jnp.int32)
    spots = ids[:, :1] * leaf + ids[:, 1:2]
    return dot(one_hot(spots == iota((ids.shape[0], emb.shape[0]), 1)), emb[...]).astype(BF16)


def picked_of(nodes, parents, table, leaves, rank):
    rows = jnp.concatenate(
        [table[:rank, leaves + q - 1 : leaves + q] + 2 * rank * (q - parents) for q in range(parents, 2 * parents)], axis=0
    )
    return dot(one_hot(rows == iota((parents * rank, nodes.shape[0]), 1)), nodes).astype(BF16)


def pre_body(leaves, *refs):
    sources, (payload, rhs_tree, weights), targets, sems = refs[:7], refs[7:10], refs[10:17], refs[17]
    copies = fetch(sources, targets, sems)
    order, skel, pick, rhs, basis, transfer, emb = targets
    cols, items = rhs.shape
    leaf = items // leaves
    rank = skel.shape[1]
    blocks = items // leaf
    for copy in copies[:6]:
        copy.wait()
    table = padded_columns([skel[...], pick[...]], 16)
    joined = jnp.concatenate([rhs[:, b * leaf : (b + 1) * leaf] for b in range(blocks)], axis=0)

    def gather(l):
        row = jnp.concatenate([order_row(order, l + j) for j in range(8)], axis=1)
        low, high = row & (leaf - 1), row // leaf
        found = dot(joined, one_hot(low == iota((leaf, 8 * leaf), 0)))
        total = None
        for b in range(blocks):
            part = jnp.where(high == b, found[b * cols : (b + 1) * cols, :], 0.0)
            total = part if total is None else total + part
        picked = total.astype(BF16)
        rhs_tree[:, l * leaf : (l + 8) * leaf] = picked
        found = []
        for j in range(8):
            lanes = slice((l + j) * leaf, (l + j + 1) * leaf)
            found.append(dot_last(basis[:, lanes], picked[:, j * leaf : (j + 1) * leaf]))
            weights[(l + j) * rank : (l + j + 1) * rank, :] = found[-1]
        return found

    def lift(q, left, right):
        pair = jnp.concatenate([left, right], axis=0)
        return dot_first_right(transfer[2 * q - 1 : 2 * q + 1].reshape(2 * rank, rank), pair)

    nodes, parents, pending = None, leaves, {}
    for l in range(leaves):
        if l % 8 == 0:
            group = gather(l)
        node, q = group[l % 8], leaves + l
        if l == 1:
            copies[6].wait()
        if l == leaves - 1:
            nodes = items_of(nodes, leaf, emb)
        while q % 2:
            node = lift(q // 2, pending.pop(q - 1), node)
            q //= 2
            if q == 1:
                break
        pending[q] = node
        if nodes is None:
            nodes = skeleton_ids(leaves, leaf, order, table, rank)
        elif parents > 1:
            parents //= 2
            nodes = picked_of(nodes, parents, table, leaves, rank)
    while parents > 1:
        parents //= 2
        nodes = picked_of(nodes, parents, table, leaves, rank)
    own = pending[1]
    share = dot_first_right(transfer[0], own)
    payload[...] = jnp.concatenate([nodes, own.astype(BF16), share.astype(BF16)], axis=1)


def packed(weights, width):
    rank, cols = weights.shape
    rows = rank * cols // width
    return jnp.concatenate([weights[r : r + rows, :] for r in range(0, rank, rows)], axis=1)


def send(payload, points, weights):
    rank, width = points.shape
    points = points.astype(BF16)
    tail = packed(weights, width).astype(BF16)
    for r in range(payload.shape[0]):
        payload[r, :rank, :] = points
        payload[r, rank:, :] = tail


def side_body(rank, me_ref, mine, pick, hot, kept):
    me = me_ref[0]
    devices = pick.shape[1]
    parent = one_hot(iota((8, devices), 1) == (devices + me) // 2)
    spots = dot_last(pick[...].astype(F32).astype(BF16), parent)[:, :1].astype(jnp.int32)
    shift = jnp.where(me % 2 == 0, 0, rank)
    spots = jnp.where(spots >= shift, spots - shift, spots + rank)
    hot[...] = one_hot(spots == iota((rank, 2 * rank), 1))
    kept[...] = mine[...]


def pair_body(rank, cols, hot, mine, other, payload, pairs, siblings):
    width = mine.shape[1] - 2 * cols
    both = jnp.concatenate([mine[:, :width], other[:, :width]], axis=0)
    pairs[...] = both
    siblings[...] = other[:, width : width + cols].astype(F32)
    total = mine[:, width + cols :].astype(F32) + other[:, width + cols :].astype(F32)
    send(payload, dot(hot[...], both), total)


def slots_of(radix):
    starts, at = [], 0
    for h in range(radix.bit_length()):
        starts.append(at)
        at += radix >> h
    return starts


def prep_body(devices, radices, me_ref, pick_hbm, upper_hbm, local_hbm, *refs):
    selects, lifts, chains, select_all, lift_all, pick, upper, own_transfer, rows_of, sems = refs
    copies = fetch((pick_hbm, upper_hbm, local_hbm.at[pl.ds(0, 1)]), (pick, upper, own_transfer), sems)
    rank = own_transfer.shape[1]
    me = me_ref[0]
    most = max(radices)
    slots = 2 * most
    nodes = slots * len(radices)
    here = iota((nodes, devices), 0)
    wanted = jnp.full((nodes, devices), -1, jnp.int32)
    base = 1
    for stage, radix in enumerate(radices):
        depth = radix.bit_length() - 1
        top = (devices + me) // (1 << (base + depth))
        for h, start in enumerate(slots_of(radix)):
            first = stage * slots + start
            inside = (here >= first) & (here < first + (radix >> h))
            wanted = jnp.where(inside, here - first + top * (radix >> h), wanted)
        base += depth
    hot = one_hot(wanted == iota((nodes, devices), 1))
    for copy in copies:
        copy.wait()
    table = dot_last(pick[...].astype(F32).astype(BF16), hot).astype(jnp.int32)
    flat = dot_last(hot, upper[...].reshape(rank * rank, devices))
    for a in range(rank):
        rows_of[a * nodes : (a + 1) * nodes, :] = flat[:, a * rank : (a + 1) * rank]

    def moved_of(slot):
        return rows_of[pl.ds(slot, rank, stride=nodes), :]

    base = 1
    chain = own_transfer[0].astype(F32)
    for stage, radix in enumerate(radices):
        depth = radix.bit_length() - 1
        place = (me // (1 << base)) % radix
        wide = radix * rank
        starts = [rank * s for s in slots_of(radix)]
        eye = iota((wide, wide), 0) == iota((wide, wide), 1)
        select_all[0:wide, :wide] = jnp.where(eye, 1.0, 0.0)
        lift_all[0:wide, :wide] = jnp.where(eye, 1.0, 0.0)
        for h in range(1, depth + 1):
            below, at = starts[h - 1], starts[h]
            for p in range(radix >> h):
                pair = slice(below + 2 * rank * p, below + 2 * rank * (p + 1))
                spot = slice(at + rank * p, at + rank * (p + 1))
                slot = stage * slots + at // rank + p
                picked = one_hot(table[:, slot : slot + 1] == iota((rank, 2 * rank), 1))
                select_all[spot, :wide] = dot(picked, select_all[pair, :wide].astype(BF16))
                child = stage * slots + below // rank + 2 * p
                moved = jnp.concatenate([moved_of(child), moved_of(child + 1)], axis=0).astype(BF16)
                lift_all[spot, :wide] = dot_first_right(moved, lift_all[pair, :wide])
        steps = [place // (1 << h) for h in range(depth)]
        mine = [pl.multiple_of(starts[h] + rank * s, rank) for h, s in enumerate(steps)]
        others = [pl.multiple_of(starts[h] + rank * (s + 1 - 2 * (s % 2)), rank) for h, s in enumerate(steps)]
        for i, spot in enumerate(mine + others + [starts[depth]]):
            selects[stage, i * rank : (i + 1) * rank, :wide] = select_all[pl.ds(spot, rank), :wide].astype(BF16)
        for i, spot in enumerate(others + [starts[depth]]):
            high, low = split(lift_all[pl.ds(spot, rank), :wide])
            lifts[stage, 0, i * rank : (i + 1) * rank, :wide] = high
            lifts[stage, 1, i * rank : (i + 1) * rank, :wide] = low
        for h in range(depth):
            step = moved_of(stage * slots + starts[h] // rank + steps[h]).astype(BF16)
            chains[stage, h * rank : (h + 1) * rank, :] = chain
            high, low = split(chain)
            chain = dot(high, step) + dot(low, step)
        base += depth


def gathered_nodes(rank, cols, gathered, select, lift, turned=False):
    count, rows, width = gathered.shape
    wide = count * rank
    places = range(count)[::-1] if turned else range(count)
    points = dot(select[:, :wide], jnp.concatenate([gathered[j, :rank, :] for j in places], axis=0)).astype(BF16)
    tails = gathered[:, rank:, :].astype(F32)
    parts = [tails[j, :, c : c + cols] for j in places for c in range(0, width, cols)]
    weights = jnp.concatenate(parts, axis=0).astype(BF16)
    return points, dot(lift[0, :, :wide], weights) + dot(lift[1, :, :wide], weights)


def terms_of(own, other, weights, rank):
    count, width = own.shape
    gram = dot_last(own, other)
    own_wide, other_wide = own.astype(F32), other.astype(F32)
    across = jnp.sum(own_wide * own_wide, axis=1, keepdims=True)
    down = jnp.sum(other_wide * other_wide, axis=1, keepdims=True)
    down = jnp.broadcast_to(down, (count, 128)).T[0:1, :]
    kernel = kernel_of(across + down - 2.0 * gram, width)
    same = iota(gram.shape, 0) // rank == iota(gram.shape, 1) // rank
    return dot_wide(jnp.where(same, kernel, 0.0), weights)


def chained(chain, terms, rank):
    total = None
    for h in range(terms.shape[0] // rank):
        part = dot_wide(chain[h * rank : (h + 1) * rank, :], terms[h * rank : (h + 1) * rank, :])
        total = part if total is None else total + part
    return total


def hop_body(stage, depth, rank, cols, gathered, selects, lifts, payload, pairs, siblings):
    rows = depth * rank
    points, lifted = gathered_nodes(
        rank, cols, gathered, selects[stage, : (2 * depth + 1) * rank, :], lifts[stage, :, : rows + rank, :]
    )
    pairs[...] = points[: 2 * rows, :]
    siblings[...] = lifted[:rows, :]
    send(payload, points[2 * rows :, :], lifted[rows:, :])


def terms_body(depths, rank, chains, *refs):
    total = terms_of(refs[0][:rank, :], refs[0][rank:, :], refs[1][...], rank)
    for stage, depth in enumerate(depths):
        pairs, siblings = refs[2 * stage + 2], refs[2 * stage + 3]
        rows = depth * rank
        terms = terms_of(pairs[:rows, :], pairs[rows:, :], siblings[...], rank)
        total = total + chained(chains[stage], terms, rank)
    refs[-1][...] = total


def final_body(stage, depth, rank, cols, gathered, selects, lifts, chains, before, spread, product):
    rows = depth * rank
    points, lifted = gathered_nodes(
        rank, cols, gathered, selects[stage, : 2 * rows, :], lifts[stage, :, :rows, :], turned=True
    )
    terms = terms_of(points[:rows, :], points[rows:, :], lifted, rank)
    field = chained(chains[stage], terms, rank) + before[...]
    high = field.astype(BF16).astype(F32)
    low = field - high
    eye = jnp.where(iota((cols, cols), 0) == iota((cols, cols), 1), 1.0, 0.0)
    right = jnp.concatenate([eye, eye, high, high, low, jnp.zeros_like(low)], axis=0).astype(BF16)
    product[...] = dot_first(right, spread[...]).astype(BF16)


def far_body(leaves, parts, rank, cols, pick, weights, transfer, *refs):
    count = leaves
    terms = []
    table = padded_columns([pick[...]], 8)
    points = jnp.concatenate([ref[...] for ref in refs[:parts]], axis=0)
    result = refs[parts]
    level = weights[...]
    while count > 1:
        kernel, _ = self_kernel(points)
        here = iota(kernel.shape, 0) // rank
        there = iota(kernel.shape, 1) // rank
        partner = here + 1 - 2 * (here % 2)
        terms.append(dot_wide(jnp.where(there == partner, kernel, 0.0), level))
        half = count // 2
        if half > 1:
            points = picked_of(points, half, table, 0, rank)
            level = jnp.concatenate(
                [
                    dot_first_right(
                        transfer[2 * q - 1 : 2 * q + 1].reshape(2 * rank, rank),
                        level[2 * rank * (q - half) : 2 * rank * (q - half + 1), :],
                    )
                    for q in range(half, 2 * half)
                ],
                axis=0,
            )
        count = half
    below = None
    for height in reversed(range(len(terms))):
        count = leaves >> height
        nodes = []
        for n in range(count):
            moved = transfer[count + n - 1]
            term = terms[height][n * rank : (n + 1) * rank, :]
            if below is None:
                node = jnp.concatenate([term, moved.astype(F32), jnp.zeros((rank, 128 - cols - rank), F32)], axis=1)
            else:
                pad = jnp.zeros((rank, 128 - cols), F32)
                node = dot_right(moved, below[n // 2]) + jnp.concatenate([term, pad], axis=1)
            nodes.append(node)
        below = nodes
    result[...] = jnp.concatenate(below, axis=0)


def leaf_body(first, count, rank, order, emb, rhs_tree, skel, near, points):
    items = emb.shape[0]
    leaf = near.shape[1] // count
    table = padded_columns([skel[...]], 8)
    turned = emb[...].T
    for i in range(0, count, 4):
        row = jnp.concatenate([order_row(order, first + j) for j in range(i, i + 4)], axis=1)
        offset = one_hot(iota((leaf, 4 * leaf), 0) == (row & (leaf - 1)))
        block = jnp.broadcast_to(digits_of(row, leaf)[0], (leaf, 4 * leaf))
        hot = jnp.concatenate([jnp.where(block == b, offset, jnp.zeros_like(offset)) for b in range(items // leaf)], axis=0)
        both = dot(turned, hot).astype(BF16)
        for j in range(i, i + 4):
            l = first + j
            feats = both[:, (j - i) * leaf : (j - i + 1) * leaf].astype(F32).T.astype(BF16)
            kernel, eye = self_kernel(feats)
            kernel = jnp.where(eye, kernel + RIDGE, kernel).astype(BF16)
            near[:, j * leaf : (j + 1) * leaf] = dot(rhs_tree[:, l * leaf : (l + 1) * leaf], kernel)
            spots = one_hot(table[:rank, l : l + 1] == iota((rank, leaf), 1))
            points[j * rank : (j + 1) * rank, :] = dot(spots, feats).astype(BF16)


def spread_body(parts, leaf, rank, order, basis, far, *refs):
    near, result, tree, offset, block = refs[:parts], refs[parts], refs[parts + 1], refs[parts + 2], refs[parts + 3]
    items = basis.shape[1]
    cols = near[0].shape[0]
    order_t = columns_of(order[...])
    for c in range(order.shape[0]):
        column = order_t[:, c : c + 1]
        rows = slice(c * 128, (c + 1) * 128)
        offset[rows, :] = one_hot(iota((128, leaf), 1) == (column & (leaf - 1)))
        block[rows, :] = jnp.broadcast_to(digits_of(column, leaf)[0], (128, leaf))
    l = 0
    for part in near:
        for i in range(part.shape[1] // leaf):
            lanes = slice(l * leaf, (l + 1) * leaf)
            high, low = split(far[l * rank : (l + 1) * rank, :])
            both = dot_first(high, basis[:, lanes]) + dot_first(low, basis[:, lanes])
            total = part[:, i * leaf : (i + 1) * leaf] + both[:cols, :]
            total_high = total.astype(BF16).astype(F32)
            moved = both[cols : cols + rank, :]
            moved_high = moved.astype(BF16).astype(F32)
            tree[:, lanes] = jnp.concatenate(
                [total_high, total - total_high, moved_high, moved - moved_high, moved_high, jnp.zeros_like(moved)], axis=0
            ).astype(BF16)
            l += 1
    for b in range(items // leaf):
        hot = jnp.where(block[...] == b, offset[...], jnp.zeros_like(offset))
        result[:, b * leaf : (b + 1) * leaf] = dot(tree[...], hot).astype(BF16)


def call(body, outs, scratch=(), flops=1e8, name=None, specs=None, limit=VMEM_LIMIT):
    extra = {} if specs is None else {"in_specs": specs}
    return pl.pallas_call(
        body,
        out_shape=outs,
        scratch_shapes=list(scratch),
        cost_estimate=pl.CostEstimate(flops=int(flops), bytes_accessed=1 << 20, transcendentals=0),
        compiler_params=pltpu.CompilerParams(vmem_limit_bytes=limit),
        name=name,
        **extra,
    )


def after(values, earlier):
    return lax.optimization_barrier((*values, earlier))[:-1]


def shape(dims, dtype):
    return jax.ShapeDtypeStruct(dims, dtype)


def local(
    embeddings,
    rhs,
    item_order,
    leaf_basis,
    leaf_skel,
    local_transfer,
    local_pick,
    upper_transfer,
    upper_pick,
):
    leaves, rank = leaf_skel.shape
    items, cols = rhs.shape
    width = embeddings.shape[1]
    devices = lax.axis_size("leaf")
    radices = RADICES[devices]
    me = lax.axis_index("leaf")
    me = me.astype(jnp.int32).reshape(1)
    order = item_order.reshape(items // 128, 128)
    basis_t = leaf_basis.T
    far_away = pl.BlockSpec(memory_space=pltpu.HBM)

    given = (order, leaf_skel, local_pick, rhs.T, basis_t, local_transfer, embeddings)
    payload, rhs_tree, weights = call(
        functools.partial(pre_body, leaves),
        (
            shape((rank, width + 2 * cols), BF16),
            shape((cols, items), BF16),
            shape((leaves * rank, cols), F32),
        ),
        scratch=[pltpu.VMEM(x.shape, x.dtype) for x in given] + [pltpu.SemaphoreType.DMA((len(given),))],
        specs=[far_away] * len(given),
        limit=ALL_VMEM,
        name="pre",
    )(*given)
    other = lax.ppermute(payload, "leaf", [(i, i ^ 1) for i in range(devices)])
    memory = pl.BlockSpec(memory_space=pltpu.SMEM)
    whole = pl.BlockSpec(memory_space=pltpu.VMEM)
    hot, kept = call(
        functools.partial(side_body, rank),
        (shape((rank, 2 * rank), BF16), shape(payload.shape, BF16)),
        specs=[memory] + [whole] * 2,
        name="side",
    )(me, payload, upper_pick.T)
    sent = rank + rank * cols // width
    payload, pairs, siblings = call(
        functools.partial(pair_body, rank, cols),
        (
            shape((radices[0], sent, width), BF16),
            shape((2 * rank, width), BF16),
            shape((rank, cols), F32),
        ),
        name="pair",
    )(hot, kept, other)
    held = [pairs, siblings]

    stages = len(radices)
    most = max(radices)
    depths = [n.bit_length() - 1 for n in radices]
    deepest = max(depths)
    nodes = 2 * most * stages
    (me,) = after((me,), payload)
    selects, lifts, chains = call(
        functools.partial(prep_body, devices, radices),
        (
            shape((stages, (2 * deepest + 1) * rank, most * rank), BF16),
            shape((stages, 2, (deepest + 1) * rank, most * rank), BF16),
            shape((stages, deepest * rank, rank), F32),
        ),
        scratch=[
            pltpu.VMEM((2 * most * rank, most * rank), F32),
            pltpu.VMEM((2 * most * rank, most * rank), F32),
            pltpu.VMEM((rank, devices), jnp.int32),
            pltpu.VMEM((rank, rank, devices), BF16),
            pltpu.VMEM((1, rank, rank), BF16),
            pltpu.VMEM((rank * nodes, rank), F32),
            pltpu.SemaphoreType.DMA((3,)),
        ],
        specs=[memory] + [far_away] * 3,
        flops=2e9,
        name="prep",
    )(me, upper_pick.T, upper_transfer.transpose(1, 2, 0), local_transfer)

    def leaf_part(first, count, earlier):
        return call(
            functools.partial(leaf_body, first, count, rank),
            (shape((cols, items // leaves * count), F32), shape((count * rank, width), BF16)),
            flops=2e9,
            name="leaf",
        )(after((order,), earlier)[0], embeddings, rhs_tree, leaf_skel)

    lead = leaves // 2
    parts = [leaf_part(0, lead, chains)]
    base = 1
    for stage, (n, depth) in enumerate(zip(radices, depths)):
        stride = 1 << base
        groups = [
            [high * stride * n + low + stride * j for j in (range(n) if stage + 1 < stages else range(n)[::-1])]
            for high in range(devices // (stride * n))
            for low in range(stride)
        ]
        gathered = lax.all_to_all(payload, "leaf", 0, 0, axis_index_groups=groups)
        base += depth
        if stage == 1:
            parts.append(leaf_part(lead, leaves - lead, payload))
        if stage + 1 < stages:
            gathered, *held_points = lax.optimization_barrier((gathered, *parts[-1]))
            parts[-1] = held_points
        if stage + 1 < stages:
            payload, pairs, siblings = call(
                functools.partial(hop_body, stage, depth, rank, cols),
                (
                    shape((radices[stage + 1], sent, width), BF16),
                    shape((2 * depth * rank, width), BF16),
                    shape((depth * rank, cols), F32),
                ),
                name="hop",
            )(gathered, selects, lifts)
            held += [pairs, siblings]
    chains_last, far_weights = after((chains, weights), payload)
    far = call(
        functools.partial(far_body, leaves, len(parts), rank, cols),
        shape((leaves * rank, 128), F32),
        flops=1e9,
        name="far",
    )(local_pick, far_weights, local_transfer, *[part[1] for part in parts])
    spread = call(
        functools.partial(spread_body, len(parts), items // leaves, rank),
        shape((256, items), BF16),
        scratch=[
            pltpu.VMEM((256, items), BF16),
            pltpu.VMEM((items, items // leaves), BF16),
            pltpu.VMEM((items, items // leaves), BF16),
        ],
        flops=2e9,
        name="spread",
    )(order, basis_t, far, *[part[0] for part in parts])
    field = call(functools.partial(terms_body, depths[:-1], rank), shape((rank, cols), F32), name="terms")(chains_last, *held)
    product = call(
        functools.partial(final_body, stages - 1, depths[-1], rank, cols), shape((cols, items), BF16), name="final"
    )(gathered, selects, lifts, chains, field, spread)
    return product.T


def solution(mesh):
    return jax.shard_map(
        local,
        mesh=mesh,
        in_specs=(
            P("leaf", None),
            P("leaf", None),
            P("leaf"),
            P("leaf", None),
            P("leaf", None),
            P("leaf", None, None),
            P("leaf", None),
            P(),
            P(),
        ),
        out_specs=P("leaf", None),
        check_vma=False,
    )
```
